32 devices in a mesh: lower: 4 (over y, core), upper: 2 (over x), depth: 4 (over z).
Axes of the slice: x: 2, y: 2, z: 4, core: 2. Of those that a mesh axis runs over, the one named last changes fastest.
Arguments:
- lower_vectors: bfloat16 [4, 32768, 512], P('depth', 'lower', 'upper'), may hold values from -0.0234375 to 0.0234375
- upper_vectors: bfloat16 [4, 32768, 768], P('depth', 'lower', 'upper'), may hold values from -6 to 6
- energy_lower: float32 [512], P(('lower', 'depth')), may hold values from 0 to 0.5
- energy_upper: float32 [768], P('upper'), may hold values from 1 to 2
- sym_lower: int32 [512], P(('lower', 'depth')), may hold values from 0 to 3
- sym_upper: int32 [768], P('upper'), may hold values from 0 to 3
- j_lower: int32 [512], P(('lower', 'depth')), may hold values from 0 to 2
- j_upper: int32 [768], P('upper'), may hold values from 0 to 2
Outputs:
- einstein: float32 [512, 768], P(('lower', 'depth'), 'upper')
The draws below stay inside these ranges and needn't reach their ends.
All inputs are finite; a program needn't handle non-finite values.
Results may differ from the reference program's by a relative error of at most 0.0003.
Values may be sent and summed in bfloat16 or wider, within the bound.
No kernel may reach another device: no remote copies, remote signals or barrier semaphores. Data moves between devices by JAX's collectives and lax.ppermute only.
A program may use at most 64 MiB of HBM per device.

```python
import jax
import jax.numpy as jnp
from jax import lax

BASIS = 131072
NL = 512
NU = 768
SLAB = 32768
N_DEPTH = 4


def set_ends(values, key, least, largest):
    longest = values.shape.index(max(values.shape))
    spots = []
    for shift in (0, 1):
        where = [jax.random.randint(jax.random.fold_in(key, axis), (), 0, length) for axis, length in enumerate(values.shape)]
        where[longest] = (where[longest] + shift) % values.shape[longest]
        spots.append(tuple(where))
    return values.at[spots[0]].set(least).at[spots[1]].set(largest)


def strengthened(entries, own_key, source, target, blocks, factor):
    def block_of(axis_at):
        return (jnp.arange(entries.shape[axis_at]) // (entries.shape[axis_at] // blocks)).reshape((-1,) + (1,) * (entries.ndim - 1 - axis_at))

    near = jax.random.permutation(own_key, blocks)[block_of(target)]
    far = (block_of(target) + blocks // 2) % blocks
    return jnp.where((block_of(source) == near) | (block_of(source) == far), factor * entries, entries)


def steps_of(stream_key, shape, split, least, high):
    loudness, own = 1.0, jax.random.fold_in(stream_key, 6)
    for dim, parts in split:
        draws = jnp.exp(jax.random.uniform(jax.random.fold_in(own, dim), (parts,), jnp.float32, least / len(split), high / len(split)))
        loudness = loudness * jnp.repeat(draws, shape[dim] // parts).reshape([-1 if axis == dim else 1 for axis in range(len(shape))])
    return loudness


def scatter_about(key, shape, spread, most, shards=(), kind=jnp.bfloat16):
    array = spread * jax.random.normal(key, shape, jnp.float32)
    if shards:
        array = array * steps_of(key, shape, shards, -0.22, 0.18)
    return jnp.clip(array, -most, most).astype(kind)


def heavy_noise(own_key, extent, scale, most, pieces, heavy, held_as=jnp.bfloat16):
    result = scale * jax.random.normal(own_key, extent, jnp.float32)
    if pieces:
        result = result * steps_of(own_key, extent, pieces, -0.22, 0.18)
    return jnp.clip(strengthened(result, jax.random.fold_in(own_key, 3), *heavy), -most, most).astype(held_as)


def setup_inputs(seed: int = 0) -> dict:
    keys = jax.random.split(jax.random.key(seed), 9)
    lower_vectors = heavy_noise(keys[0], (N_DEPTH, SLAB, NL), BASIS ** -0.5, 0.0234375, ((0, 4), (1, 4), (2, 2)), (1, 2, 4, 2.0))
    upper_vectors = scatter_about(keys[1], (N_DEPTH, SLAB, NU), 1.0, 6.0, ((0, 4), (1, 4), (2, 2)))
    energy_lower = jnp.clip(0.5 * jax.random.uniform(keys[2], (NL,), jnp.float32) ** steps_of(keys[2], (NL,), ((0, 16),), -0.2, 0.2), 0.0, 0.5)
    energy_upper = jnp.clip(1.0 + 1.0 * jax.random.uniform(keys[3], (NU,), jnp.float32) ** steps_of(keys[3], (NU,), ((0, 2),), -0.2, 0.2), 1.0, 2.0)
    sym_lower = set_ends(jax.random.randint(keys[4], (NL,), 0, 4), jax.random.fold_in(keys[4], 1), 0, 3).astype(jnp.int32)
    sym_upper = set_ends(jax.random.randint(keys[5], (NU,), 0, 4), jax.random.fold_in(keys[5], 1), 0, 3).astype(jnp.int32)
    j_lower = set_ends(jax.random.randint(keys[6], (NL,), 0, 3), jax.random.fold_in(keys[6], 1), 0, 2).astype(jnp.int32)
    j_upper = set_ends(jax.random.randint(keys[7], (NU,), 0, 3), jax.random.fold_in(keys[7], 1), 0, 2).astype(jnp.int32)
    return dict(lower_vectors=lower_vectors, upper_vectors=upper_vectors, energy_lower=energy_lower, energy_upper=energy_upper, sym_lower=sym_lower, sym_upper=sym_upper, j_lower=j_lower, j_upper=j_upper)


def reference(lower_vectors, upper_vectors, energy_lower, energy_upper, sym_lower, sym_upper, j_lower, j_upper):
    moments = jnp.zeros((NL, NU), jnp.float32)
    for slab_index in range(N_DEPTH):
        lower_slab = lower_vectors[slab_index].astype(jnp.float32)
        upper_slab = upper_vectors[slab_index].astype(jnp.float32)
        moments = moments + lax.dot_general(lower_slab, upper_slab, (((0,), (0,)), ((), ())), precision=lax.Precision.HIGHEST, preferred_element_type=jnp.float32)
    parity = sym_lower % 2
    sym_rule = (sym_upper[None, :] - sym_lower[:, None]) == (1 - 2 * parity)[:, None]
    j_rule = jnp.abs(j_upper[None, :] - j_lower[:, None]) <= 1
    allowed = jnp.logical_and(sym_rule, j_rule)
    frequency = energy_upper[None, :] - energy_lower[:, None]
    weight_upper = (2 * j_upper + 1).astype(jnp.float32)
    value = frequency * frequency * frequency * (moments * moments) / weight_upper[None, :]
    return jnp.where(allowed, value, jnp.zeros_like(value))
```

```python
import jax
import jax.numpy as jnp
from jax import lax
from jax.experimental import pallas as pl
from jax.experimental.pallas import tpu as pltpu
from jax.sharding import PartitionSpec as P

OWNERS = ("lower", "depth")
VMEM_LIMIT = 16 * 1024 * 1024


def params():
    return pltpu.CompilerParams(vmem_limit_bytes=VMEM_LIMIT)


def cost():
    return pl.CostEstimate(flops=1024, bytes_accessed=1024, transcendentals=0)


def dot(a, b):
    return jnp.dot(a, b, preferred_element_type=jnp.float32)


def after(x, *others):
    return lax.optimization_barrier((x,) + others)[0]


def in_hbm(x):
    return pltpu.with_memory_space_constraint(x, pltpu.HBM)


def whole(shape):
    return pl.BlockSpec(shape, lambda *_: (0,) * len(shape))


def turn(lower_rows, heads, pieces, unit, mine, n_dep):
    rows, cols = lower_rows.shape
    per_block = cols // mine
    kind = lower_rows.dtype
    block = 2 * unit
    skipped = heads // block
    steps = (rows - heads) // block

    def body(low, *outs):
        i = pl.program_id(0)
        flipped = low[...].astype(jnp.float32).T
        by_owner = flipped.reshape(per_block, mine, block)
        for (start, stop, begin, end), out in zip(pieces, outs):

            @pl.when((i >= begin // 2) & (i < end // 2))
            def _():
                out[...] = by_owner[:, start:stop].reshape(per_block * (stop - start), block).astype(kind)

        @pl.when(i == steps - 1)
        def _():
            by_depth = flipped.reshape(per_block // n_dep, n_dep, mine, block)
            for z in range(n_dep):
                outs[-1][z] = by_depth[:, z].reshape(cols // n_dep, block).astype(kind)

    def spec(start, stop, begin, end):
        return pl.BlockSpec(
            (per_block * (stop - start), block),
            lambda i: (0, jnp.clip(i - begin // 2, 0, (end - begin) // 2 - 1)),
        )

    tail_shape = (n_dep, cols // n_dep, block)
    return pl.pallas_call(
        body,
        grid=(steps,),
        in_specs=[pl.BlockSpec((block, cols), lambda i: (i + skipped, 0))],
        out_specs=[spec(*piece) for piece in pieces] + [whole(tail_shape)],
        out_shape=[
            jax.ShapeDtypeStruct((per_block * (stop - start), (end - begin) * unit), kind)
            for start, stop, begin, end in pieces
        ]
        + [jax.ShapeDtypeStruct(tail_shape, kind)],
        compiler_params=params(),
        cost_estimate=cost(),
    )(in_hbm(lower_rows))


def split_states(product, per_block, parts):
    states, width = product.shape
    by_owner = product.reshape(per_block, parts, states // per_block // parts, width)
    return [by_owner[:, i].reshape(states // parts, width) for i in range(parts)]


def own_product(slot, lower_rows, upper_rows, n_up, per_block, parts):
    rows, cols = lower_rows.shape
    width = upper_rows.shape[1]
    steps = 4
    block = rows // steps

    def body(at, low, up, *refs):
        outs, total = refs[:-1], refs[-1]
        i = pl.program_id(0)
        term = dot(low[...].T, up[...])

        @pl.when(i == 0)
        def _():
            total[...] = term

        @pl.when(i > 0)
        def _():
            total[...] += term

        @pl.when(i == steps - 1)
        def _():
            for out, part in zip(outs, split_states(total[...], per_block, parts)):
                out[0] = part

    return pl.pallas_call(
        body,
        grid_spec=pltpu.PrefetchScalarGridSpec(
            num_scalar_prefetch=1,
            grid=(steps,),
            in_specs=[
                pl.BlockSpec((block, cols), lambda i, at: (i, 0)),
                pl.BlockSpec((block, width), lambda i, at: (i, 0)),
            ],
            out_specs=[pl.BlockSpec((1, cols // parts, width), lambda i, at: (at[0], 0, 0))] * parts,
            scratch_shapes=[pltpu.VMEM((cols, width), jnp.float32)],
        ),
        out_shape=[jax.ShapeDtypeStruct((n_up, cols // parts, width), jnp.float32)] * parts,
        compiler_params=params(),
        cost_estimate=cost(),
    )(slot.reshape(1), in_hbm(lower_rows), in_hbm(upper_rows))


def rows_product(got, upper_rows, first, so_far, per_block, parts):
    k, states = got.shape
    width = upper_rows.shape[1]

    def body(low, up, *refs):
        outs = refs[-parts:]
        for i, part in enumerate(split_states(dot(low[...].T, up[...]), per_block, parts)):
            outs[i][...] = part + refs[i][...] if so_far else part

    shape = (states // parts, width)
    return pl.pallas_call(
        body,
        grid=(1,),
        in_specs=[whole((k, states)), pl.BlockSpec((k, width), lambda i: (first // k, 0))]
        + [whole(shape)] * len(so_far),
        out_specs=[whole(shape)] * parts,
        out_shape=[jax.ShapeDtypeStruct(shape, jnp.float32)] * parts,
        compiler_params=params(),
        cost_estimate=cost(),
    )(got, in_hbm(upper_rows), *so_far)


def turned_product(got, upper_rows, first, block, so_far):
    states, k = got.shape
    width = upper_rows.shape[1]

    def body(low, up, before, out):
        term = dot(low[...], up[...])

        @pl.when(pl.program_id(0) == 0)
        def _():
            out[...] = before[...] + term

        @pl.when(pl.program_id(0) > 0)
        def _():
            out[...] += term

    return pl.pallas_call(
        body,
        grid=(k // block,),
        in_specs=[
            pl.BlockSpec((states, block), lambda i: (0, i)),
            pl.BlockSpec((block, width), lambda i: (i + first // block, 0)),
            whole((states, width)),
        ],
        out_specs=whole((states, width)),
        out_shape=jax.ShapeDtypeStruct((states, width), jnp.float32),
        compiler_params=params(),
        cost_estimate=cost(),
    )(got, in_hbm(upper_rows), so_far)


def last_product(slot, got, upper_rows, first, so_far, buffer):
    states, k = got.shape
    width = upper_rows.shape[1]

    def body(at, low, up, before, _, out):
        out[0] = before[...] + dot(low[...], up[...])

    return pl.pallas_call(
        body,
        grid_spec=pltpu.PrefetchScalarGridSpec(
            num_scalar_prefetch=1,
            grid=(1,),
            in_specs=[
                whole((states, k)),
                pl.BlockSpec((k, width), lambda i, at: (first // k, 0)),
                whole((states, width)),
                pl.BlockSpec(memory_space=pl.ANY),
            ],
            out_specs=pl.BlockSpec((1, states, width), lambda i, at: (at[0], 0, 0)),
        ),
        out_shape=jax.ShapeDtypeStruct(buffer.shape, buffer.dtype),
        input_output_aliases={4: 0},
        compiler_params=params(),
        cost_estimate=cost(),
    )(slot.reshape(1), got, in_hbm(upper_rows), so_far, buffer)


def tail_product(depth, got, own, forward, backward):
    n_dep, states, k = got.shape
    width = own.shape[1]
    n = len(forward)

    def body(at, low, mid, *refs):
        z = at[0]
        out = refs[-1]
        out[...] = dot(low[z], mid[...])
        for i in range(n):

            @pl.when(z > i)
            def _():
                out[...] += dot(low[z - 1 - i], refs[i][...])

            @pl.when(z + 1 + i < n_dep)
            def _():
                out[...] += dot(low[z + 1 + i], refs[n + i][...])

    vmem = pl.BlockSpec(memory_space=pltpu.VMEM)
    return pl.pallas_call(
        body,
        in_specs=[pl.BlockSpec(memory_space=pltpu.SMEM)] + [vmem] * (2 + 2 * n),
        out_specs=vmem,
        out_shape=jax.ShapeDtypeStruct((states, width), jnp.float32),
        compiler_params=params(),
        cost_estimate=cost(),
    )(depth.reshape(1), got, own, *forward, *backward)


def make_local(n_low, n_up, n_dep):
    n_owners = n_low * n_dep
    n_core = n_low // n_up
    others = range(1, n_up)

    def shifted(x, shift):
        return lax.ppermute(x, "upper", [((u + shift) % n_up, u) for u in range(n_up)])

    def low(y, c):
        return (y % n_up) * n_core + c

    def local(
        lower_vectors, upper_vectors, energy_lower, energy_upper, sym_lower, sym_upper, j_lower, j_upper
    ):
        lower_rows = lower_vectors[0]
        upper_rows = upper_vectors[0]
        rows, cols = lower_rows.shape
        width = upper_rows.shape[1]
        mine = energy_lower.shape[0]
        per_block = cols // mine
        unit = rows // 16
        heads = 4 * unit
        half = mine // 2
        pieces = ((0, half, 4, 10), (0, half, 0, 4), (half, mine, 4, 10), (half, mine, 0, 4))
        me = lax.axis_index("upper")
        depth = lax.axis_index("depth")
        my_low = lax.axis_index("lower")
        my_y, my_core = my_low // n_core, my_low % n_core

        parity = sym_lower % 2
        sym_rule = sym_upper[None, :] - sym_lower[:, None] == (1 - 2 * parity)[:, None]
        j_rule = jnp.abs(j_upper[None, :] - j_lower[:, None]) <= 1
        allowed = jnp.logical_and(sym_rule, j_rule)
        frequency = energy_upper[None, :] - energy_lower[:, None]
        weight_upper = (2 * j_upper + 1).astype(jnp.float32)
        cubed = frequency * frequency * frequency

        crossed = []

        def cross(x, *others_first):
            if len(crossed) > 1:
                x = after(x, *crossed[-2], *others_first)
            crossed.append([shifted(x, s) for s in others])

        up = [(z, z + 1) for z in range(n_dep - 1)]
        down = [(z + 1, z) for z in range(n_dep - 1)]
        forward, backward = [], []

        def pass_on(held_up, held_down):
            i = len(forward)
            forward.append(lax.ppermute(held_up, "depth", up[i:]))
            backward.append(lax.ppermute(held_down, "depth", down[: n_dep - 1 - i]))

        first = lower_rows[:heads]
        cross(first)
        later_rows = after(lower_rows, first)
        *turned, tail_rows = turn(later_rows, heads, pieces, unit, mine, n_dep)
        buffers = own_product(me, after(later_rows, turned[0]), upper_rows, n_up, per_block, 2)
        cross(after(turned[0], *buffers))
        up_tail = after(upper_rows[14 * unit :], turned[0])
        pass_on(up_tail, up_tail)
        cross(turned[1])
        for i in range(1, n_dep - 1):
            pass_on(*after((forward[-1], backward[-1]), *crossed[i - 1]))
        sorted_tail = lax.all_to_all(after(tail_rows, *crossed[1]), "depth", 0, 0)
        cross(turned[2], forward[0], backward[0])
        cross(turned[3], forward[1], backward[1], sorted_tail)
        so_far = [rows_product(g, upper_rows, 0, (), per_block, 2) for g in crossed[0]]

        def combined(i, got_1, got_2):
            buffer = buffers[i]
            for s in others:
                total = turned_product(got_1[s - 1], upper_rows, 8 * unit, 2 * unit, so_far[s - 1][i])
                slot = (me + s) % n_up
                buffer = last_product(slot, got_2[s - 1], upper_rows, heads, total, buffer)
            by_owner = buffer.reshape(n_owners, half, width)
            return buffer, jnp.sum(lax.all_to_all(by_owner, OWNERS, 0, 0), axis=0)

        _, sum_a = combined(0, crossed[1], crossed[2])
        cross(sorted_tail, forward[-1], backward[-1], sum_a)
        last, sum_b = combined(1, crossed[3], crossed[4])
        main = jnp.concatenate([sum_a, sum_b], axis=0)

        terms = [tail_product(depth, after(g, last), up_tail, forward, backward) for g in crossed[5]]

        def term_for(y):
            block = jnp.zeros_like(terms[0])
            for s in others:
                block = jnp.where((me + s) % n_up == y % n_up, terms[s - 1], block)
            return block

        tail_sum = term_for(my_y)
        for t in others:
            tail_sum = tail_sum + lax.ppermute(
                term_for(my_y + t), "lower", [(low(y, c), low(y + t, c)) for y in range(n_up) for c in range(n_core)]
            )
        by_core = tail_sum.reshape(n_core, mine, width)
        total = main + lax.dynamic_index_in_dim(by_core, my_core, 0, keepdims=False)
        for k in range(1, n_core):
            leaving = lax.dynamic_index_in_dim(by_core, (my_core + k) % n_core, 0, keepdims=False)
            total = total + lax.ppermute(
                leaving,
                "lower",
                [(low(y, c), low(y, (c + k) % n_core)) for y in range(n_up) for c in range(n_core)],
            )
        value = cubed * (total * total) / weight_upper[None, :]
        return jnp.where(allowed, value, jnp.zeros_like(value))

    return local


def solution(mesh):
    return jax.shard_map(
        make_local(mesh.shape["lower"], mesh.shape["upper"], mesh.shape["depth"]),
        mesh=mesh,
        in_specs=(
            P("depth", "lower", "upper"),
            P("depth", "lower", "upper"),
            P(("lower", "depth")),
            P("upper"),
            P(("lower", "depth")),
            P("upper"),
            P(("lower", "depth")),
            P("upper"),
        ),
        out_specs=P(("lower", "depth"), "upper"),
        check_vma=False,
    )
```

```python
import jax
import jax.numpy as jnp
from jax import lax
from jax.experimental import pallas as pl
from jax.experimental.pallas import tpu as pltpu
from jax.sharding import PartitionSpec as P

OWNERS = ("lower", "depth")
VMEM_LIMIT = 16 * 1024 * 1024


def params():
    return pltpu.CompilerParams(vmem_limit_bytes=VMEM_LIMIT)


def cost(microseconds):
    return pl.CostEstimate(flops=0, bytes_accessed=int(microseconds * 3.0e6), transcendentals=0)


def dot(a, b):
    return jnp.dot(a, b, preferred_element_type=jnp.float32)


def after(x, *others):
    return lax.optimization_barrier((x,) + others)[0]


def in_hbm(x):
    return pltpu.with_memory_space_constraint(x, pltpu.HBM)


def whole(shape):
    return pl.BlockSpec(shape, lambda *_: (0,) * len(shape))


def turn(lower_rows, parts, unit, mine, n_dep):
    rows, cols = lower_rows.shape
    per_block = cols // mine
    kind = lower_rows.dtype
    block = 2 * unit
    mains = rows // block - 2

    def body(low, *outs):
        i = pl.program_id(0)
        flipped = low[...].astype(jnp.float32).T

        @pl.when(i < mains)
        def _():
            for out, part in zip(outs, split_states(flipped, per_block, parts)):
                out[...] = part.astype(kind)

        @pl.when(i == mains)
        def _():
            by_depth = flipped.reshape(per_block // n_dep, n_dep, mine, block)
            for z in range(n_dep):
                outs[-1][z] = by_depth[:, z].reshape(cols // n_dep, block).astype(kind)

    tail_shape = (n_dep, cols // n_dep, block)
    return pl.pallas_call(
        body,
        grid=(mains + 1,),
        in_specs=[pl.BlockSpec((block, cols), lambda i: (jnp.where(i < mains, i, i + 1), 0))],
        out_specs=[pl.BlockSpec((cols // parts, block), lambda i: (0, jnp.minimum(i, mains - 1)))] * parts
        + [whole(tail_shape)],
        out_shape=[jax.ShapeDtypeStruct((cols // parts, mains * block), kind)] * parts
        + [jax.ShapeDtypeStruct(tail_shape, kind)],
        compiler_params=params(),
        cost_estimate=cost(0.01),
    )(in_hbm(lower_rows))


def split_states(product, per_block, parts):
    states, width = product.shape
    by_owner = product.reshape(per_block, parts, states // per_block // parts, width)
    return [by_owner[:, i].reshape(states // parts, width) for i in range(parts)]


def own_product(slot, lower_rows, upper_rows, n_up, per_block, parts):
    rows, cols = lower_rows.shape
    width = upper_rows.shape[1]
    steps = 4
    block = rows // steps

    def body(at, low, up, *refs):
        outs, total = refs[:-1], refs[-1]
        i = pl.program_id(0)
        term = dot(low[...].T, up[...])

        @pl.when(i == 0)
        def _():
            total[...] = term

        @pl.when(i > 0)
        def _():
            total[...] += term

        @pl.when(i == steps - 1)
        def _():
            for out, part in zip(outs, split_states(total[...], per_block, parts)):
                out[0] = part

    return pl.pallas_call(
        body,
        grid_spec=pltpu.PrefetchScalarGridSpec(
            num_scalar_prefetch=1,
            grid=(steps,),
            in_specs=[
                pl.BlockSpec((block, cols), lambda i, at: (i, 0)),
                pl.BlockSpec((block, width), lambda i, at: (i, 0)),
            ],
            out_specs=[pl.BlockSpec((1, cols // parts, width), lambda i, at: (at[0], 0, 0))] * parts,
            scratch_shapes=[pltpu.VMEM((cols, width), jnp.float32)],
        ),
        out_shape=[jax.ShapeDtypeStruct((n_up, cols // parts, width), jnp.float32)] * parts,
        compiler_params=params(),
        cost_estimate=cost(0.01),
    )(slot.reshape(1), in_hbm(lower_rows), in_hbm(upper_rows))


def rows_product(got, upper_rows, first, block, so_far, per_block, parts):
    k, states = got.shape
    width = upper_rows.shape[1]
    steps = k // block

    def body(low, up, *refs):
        outs, total = refs[-1 - parts : -1], refs[-1]
        i = pl.program_id(0)
        term = dot(low[...].T, up[...])

        @pl.when(i == 0)
        def _():
            total[...] = term

        @pl.when(i > 0)
        def _():
            total[...] += term

        @pl.when(i == steps - 1)
        def _():
            for j, part in enumerate(split_states(total[...], per_block, parts)):
                outs[j][...] = part + refs[j][...] if so_far else part

    shape = (states // parts, width)
    return pl.pallas_call(
        body,
        grid=(steps,),
        in_specs=[
            pl.BlockSpec((block, states), lambda i: (i, 0)),
            pl.BlockSpec((block, width), lambda i: (i + first // block, 0)),
        ]
        + [whole(shape)] * len(so_far),
        out_specs=[whole(shape)] * parts,
        out_shape=[jax.ShapeDtypeStruct(shape, jnp.float32)] * parts,
        scratch_shapes=[pltpu.VMEM((states, width), jnp.float32)],
        compiler_params=params(),
        cost_estimate=cost(0.01),
    )(got, in_hbm(upper_rows), *so_far)


def turned_product(slot, got, upper_rows, so_far, buffer):
    states, k = got.shape
    width = upper_rows.shape[1]
    steps = 3
    block = k // steps

    def body(at, low, up, before, _, out, total):
        i = pl.program_id(0)
        term = dot(low[...], up[...])

        @pl.when(i == 0)
        def _():
            total[...] = before[...] + term

        @pl.when((i > 0) & (i < steps - 1))
        def _():
            total[...] += term

        @pl.when(i == steps - 1)
        def _():
            out[0] = total[...] + term

    return pl.pallas_call(
        body,
        grid_spec=pltpu.PrefetchScalarGridSpec(
            num_scalar_prefetch=1,
            grid=(steps,),
            in_specs=[
                pl.BlockSpec((states, block), lambda i, at: (0, i)),
                pl.BlockSpec((block, width), lambda i, at: (i, 0)),
                whole((states, width)),
                pl.BlockSpec(memory_space=pl.ANY),
            ],
            out_specs=pl.BlockSpec((1, states, width), lambda i, at: (at[0], 0, 0)),
            scratch_shapes=[pltpu.VMEM((states, width), jnp.float32)],
        ),
        out_shape=jax.ShapeDtypeStruct(buffer.shape, buffer.dtype),
        input_output_aliases={4: 0},
        compiler_params=params(),
        cost_estimate=cost(0.01),
    )(slot.reshape(1), got, in_hbm(upper_rows), so_far, buffer)


def tail_product(depth, got, own, forward, backward):
    n_dep, states, k = got.shape
    width = own.shape[1]
    n = len(forward)

    def body(at, low, mid, *refs):
        z = at[0]
        out = refs[-1]
        out[...] = dot(low[z], mid[...])
        for i in range(n):

            @pl.when(z > i)
            def _():
                out[...] += dot(low[z - 1 - i], refs[i][...])

            @pl.when(z + 1 + i < n_dep)
            def _():
                out[...] += dot(low[z + 1 + i], refs[n + i][...])

    vmem = pl.BlockSpec(memory_space=pltpu.VMEM)
    return pl.pallas_call(
        body,
        in_specs=[pl.BlockSpec(memory_space=pltpu.SMEM)] + [vmem] * (2 + 2 * n),
        out_specs=vmem,
        out_shape=jax.ShapeDtypeStruct((states, width), jnp.float32),
        compiler_params=params(),
        cost_estimate=cost(0.01),
    )(depth.reshape(1), got, own, *forward, *backward)


def make_local(n_low, n_up, n_dep):
    n_owners = n_low * n_dep
    n_core = n_low // n_up
    others = range(1, n_up)

    def shifted(x, shift):
        return lax.ppermute(x, "upper", [((u + shift) % n_up, u) for u in range(n_up)])

    def low(y, c):
        return (y % n_up) * n_core + c

    def local(
        lower_vectors, upper_vectors, energy_lower, energy_upper, sym_lower, sym_upper, j_lower, j_upper
    ):
        lower_rows = lower_vectors[0]
        upper_rows = upper_vectors[0]
        rows, cols = lower_rows.shape
        width = upper_rows.shape[1]
        mine = energy_lower.shape[0]
        per_block = cols // mine
        unit = rows // 16
        main_rows = 12 * unit
        half = mine // 2
        me = lax.axis_index("upper")
        depth = lax.axis_index("depth")
        my_low = lax.axis_index("lower")
        my_y, my_core = my_low // n_core, my_low % n_core

        parity = sym_lower % 2
        sym_rule = sym_upper[None, :] - sym_lower[:, None] == (1 - 2 * parity)[:, None]
        j_rule = jnp.abs(j_upper[None, :] - j_lower[:, None]) <= 1
        allowed = jnp.logical_and(sym_rule, j_rule)
        frequency = energy_upper[None, :] - energy_lower[:, None]
        weight_upper = (2 * j_upper + 1).astype(jnp.float32)
        cubed = frequency * frequency * frequency

        crossed = []

        def cross(x, *others_first):
            if len(crossed) > 1:
                x = after(x, *crossed[-2], *others_first)
            crossed.append([shifted(x, s) for s in others])

        up = [(z, z + 1) for z in range(n_dep - 1)]
        down = [(z + 1, z) for z in range(n_dep - 1)]
        forward, backward = [], []

        def pass_on(held_up, held_down):
            i = len(forward)
            forward.append(lax.ppermute(held_up, "depth", up[i:]))
            backward.append(lax.ppermute(held_down, "depth", down[: n_dep - 1 - i]))

        first = lower_rows[main_rows : main_rows + 2 * unit]
        cross(first)
        later_rows = after(lower_rows, first)
        *turned, tail_rows = turn(later_rows, 2, unit, mine, n_dep)
        cross(after(turned[0], *crossed[0]))
        up_tail = after(upper_rows[main_rows + 2 * unit :], *crossed[0])
        pass_on(up_tail, up_tail)
        for i in range(1, n_dep - 1):
            pass_on(forward[-1], backward[-1])
        sorted_tail = lax.all_to_all(tail_rows, "depth", 0, 0)
        buffers = own_product(me, after(later_rows, turned[0]), upper_rows, n_up, per_block, 2)
        cross(turned[1])
        so_far = [rows_product(g, upper_rows, main_rows, 2 * unit, (), per_block, 2) for g in crossed[0]]

        def combined(i, got, *others_first):
            buffer = buffers[i]
            for s in others:
                slot = (me + s) % n_up
                buffer = turned_product(slot, got[s - 1], upper_rows, so_far[s - 1][i], buffer)
            buffer = after(buffer, *others_first) if others_first else buffer
            by_owner = buffer.reshape(n_owners, half, width)
            return buffer, jnp.sum(lax.all_to_all(by_owner, OWNERS, 0, 0), axis=0)

        _, sum_a = combined(0, crossed[1], sorted_tail)
        cross(sorted_tail, sum_a)
        last, sum_b = combined(1, crossed[2], sum_a)
        main = jnp.concatenate([sum_a, sum_b], axis=0)

        terms = [tail_product(depth, after(g, last), up_tail, forward, backward) for g in crossed[3]]

        def term_for(y):
            block = jnp.zeros_like(terms[0])
            for s in others:
                block = jnp.where((me + s) % n_up == y % n_up, terms[s - 1], block)
            return block

        total = main
        for t in range(n_up):
            by_core = term_for(my_y + t).reshape(n_core, mine, width)
            for k in range(n_core):
                term = lax.dynamic_index_in_dim(by_core, (my_core + k) % n_core, 0, keepdims=False)
                if t or k:
                    pairs = [(low(y, c), low(y + t, (c + k) % n_core)) for y in range(n_up) for c in range(n_core)]
                    term = lax.ppermute(term, "lower", pairs)
                total = total + term
        value = cubed * (total * total) / weight_upper[None, :]
        return jnp.where(allowed, value, jnp.zeros_like(value))

    return local


def solution(mesh):
    return jax.shard_map(
        make_local(mesh.shape["lower"], mesh.shape["upper"], mesh.shape["depth"]),
        mesh=mesh,
        in_specs=(
            P("depth", "lower", "upper"),
            P("depth", "lower", "upper"),
            P(("lower", "depth")),
            P("upper"),
            P(("lower", "depth")),
            P("upper"),
            P(("lower", "depth")),
            P("upper"),
        ),
        out_specs=P(("lower", "depth"), "upper"),
        check_vma=False,
    )
```

```python
import jax
import jax.numpy as jnp
from jax import lax
from jax.experimental import pallas as pl
from jax.experimental.pallas import tpu as pltpu
from jax.sharding import PartitionSpec as P

OWNERS = ("lower", "depth")
VMEM_LIMIT = 16 * 1024 * 1024


def params():
    return pltpu.CompilerParams(vmem_limit_bytes=VMEM_LIMIT)


def cost(microseconds):
    return pl.CostEstimate(flops=0, bytes_accessed=int(microseconds * 3.0e6), transcendentals=0)


def dot(a, b):
    return jnp.dot(a, b, preferred_element_type=jnp.float32)


def after(x, *others):
    return lax.optimization_barrier((x,) + others)[0]


def in_hbm(x):
    return pltpu.with_memory_space_constraint(x, pltpu.HBM)


def whole(shape):
    return pl.BlockSpec(shape, lambda *_: (0,) * len(shape))


def turn(lower_rows, parts, unit, mine, n_dep):
    rows, cols = lower_rows.shape
    per_block = cols // mine
    kind = lower_rows.dtype
    block = 2 * unit
    mains = rows // block - 2

    def body(low, *outs):
        i = pl.program_id(0)
        flipped = low[...].astype(jnp.float32).T

        @pl.when(i < mains)
        def _():
            for out, part in zip(outs, split_states(flipped, per_block, parts)):
                out[...] = part.astype(kind)

        @pl.when(i == mains)
        def _():
            by_depth = flipped.reshape(per_block // n_dep, n_dep, mine, block)
            for z in range(n_dep):
                outs[-1][z] = by_depth[:, z].reshape(cols // n_dep, block).astype(kind)

    tail_shape = (n_dep, cols // n_dep, block)
    return pl.pallas_call(
        body,
        grid=(mains + 1,),
        in_specs=[pl.BlockSpec((block, cols), lambda i: (jnp.where(i < mains, i, i + 1), 0))],
        out_specs=[pl.BlockSpec((cols // parts, block), lambda i: (0, jnp.minimum(i, mains - 1)))] * parts
        + [whole(tail_shape)],
        out_shape=[jax.ShapeDtypeStruct((cols // parts, mains * block), kind)] * parts
        + [jax.ShapeDtypeStruct(tail_shape, kind)],
        compiler_params=params(),
        cost_estimate=cost(0.01),
    )(in_hbm(lower_rows))


def split_states(product, per_block, parts):
    states, width = product.shape
    by_owner = product.reshape(per_block, parts, states // per_block // parts, width)
    return [by_owner[:, i].reshape(states // parts, width) for i in range(parts)]


def rows_product(got, upper_rows, first, block, so_far, per_block, parts):
    k, states = got.shape
    width = upper_rows.shape[1]
    steps = k // block

    def body(low, up, *refs):
        outs, total = refs[-1 - parts : -1], refs[-1]
        i = pl.program_id(0)
        term = dot(low[...].T, up[...])

        @pl.when(i == 0)
        def _():
            total[...] = term

        @pl.when(i > 0)
        def _():
            total[...] += term

        @pl.when(i == steps - 1)
        def _():
            for j, part in enumerate(split_states(total[...], per_block, parts)):
                outs[j][...] = part + refs[j][...] if so_far else part

    shape = (states // parts, width)
    return pl.pallas_call(
        body,
        grid=(steps,),
        in_specs=[
            pl.BlockSpec((block, states), lambda i: (i, 0)),
            pl.BlockSpec((block, width), lambda i: (i + first // block, 0)),
        ]
        + [whole(shape)] * len(so_far),
        out_specs=[whole(shape)] * parts,
        out_shape=[jax.ShapeDtypeStruct(shape, jnp.float32)] * parts,
        scratch_shapes=[pltpu.VMEM((states, width), jnp.float32)],
        compiler_params=params(),
        cost_estimate=cost(0.01),
    )(got, in_hbm(upper_rows), *so_far)


def turned_products(me, core, own, so_far, got, upper_rows, n_core):
    n_up = 1 + len(got)
    states, k = got[0].shape
    width = upper_rows.shape[1]
    steps = 3
    block = k // steps
    share = states // n_core

    def body(me_at, core_at, mine, up, *refs):
        befores, lows_at = refs[: n_up - 1], refs[n_up - 1 : 2 * n_up - 2]
        outs = refs[2 * n_up - 2 : 2 * n_up - 2 + n_core]
        lows, ups, sems = refs[2 * n_up - 2 + n_core :]

        def start(source, target, sem):
            copy = pltpu.make_async_copy(source, target, sem)
            copy.start()
            return copy

        copies = []
        for j in range(steps):
            span = pl.ds(j * block, block)
            copies.append(
                [start(up.at[span], ups.at[j], sems.at[0, j])]
                + [start(low.at[:, span], lows.at[i, j], sems.at[i + 1, j]) for i, low in enumerate(lows_at)]
            )

        def put(slot, product):
            by_core = product.reshape(n_core, share, width)
            for c in range(n_core):
                for t, out in enumerate(outs):

                    @pl.when(lax.rem(core_at[0] + t, n_core) == c)
                    def _():
                        out[slot] = by_core[c]

        put(me_at[0], mine[...])
        totals = [before[...] for before in befores]
        for j, group in enumerate(copies):
            for copy in group:
                copy.wait()
            totals = [total + dot(lows[i, j], ups[j]) for i, total in enumerate(totals)]
        for i, total in enumerate(totals):
            put(lax.rem(me_at[0] + 1 + i, n_up), total)

    vmem, hbm = pl.BlockSpec(memory_space=pltpu.VMEM), pl.BlockSpec(memory_space=pltpu.HBM)
    return pl.pallas_call(
        body,
        in_specs=[pl.BlockSpec(memory_space=pltpu.SMEM)] * 2 + [vmem, hbm] + [vmem] * (n_up - 1) + [hbm] * (n_up - 1),
        out_specs=[vmem] * n_core,
        out_shape=[jax.ShapeDtypeStruct((n_up, share, width), jnp.float32)] * n_core,
        scratch_shapes=[
            pltpu.VMEM((n_up - 1, steps, states, block), got[0].dtype),
            pltpu.VMEM((steps, block, width), upper_rows.dtype),
            pltpu.SemaphoreType.DMA((n_up, steps)),
        ],
        compiler_params=params(),
        cost_estimate=cost(0.01),
    )(me.reshape(1), core.reshape(1), own, in_hbm(upper_rows), *so_far, *got)


def tail_product(depth, got, own, forward, backward):
    n_dep, states, k = got.shape
    width = own.shape[1]
    n = n_dep - 1

    def body(at, low, mid, *refs):
        out, lows, ups, sems = refs[2 * n :]
        z = at[0]
        of_low = pltpu.make_async_copy(low, lows, sems.at[n_dep])
        of_low.start()
        copies = [pltpu.make_async_copy(mid, ups.at[0], sems.at[0])]
        copies[0].start()
        for j in range(1, n_dep):
            down = pltpu.make_async_copy(refs[n + j - 1], ups.at[j], sems.at[j])
            round_ = pltpu.make_async_copy(refs[n - j], ups.at[j], sems.at[j])
            pl.when(z + j < n_dep)(down.start)
            pl.when(z + j >= n_dep)(round_.start)
            copies.append(down)
        of_low.wait()
        total = jnp.zeros((states, width), jnp.float32)
        for j, copy in enumerate(copies):
            copy.wait()
            total = total + dot(lows[lax.rem(z + j, n_dep)], ups[j])
        out[...] = total

    hbm = pl.BlockSpec(memory_space=pltpu.HBM)
    return pl.pallas_call(
        body,
        in_specs=[pl.BlockSpec(memory_space=pltpu.SMEM)] + [hbm] * (2 + 2 * n),
        out_specs=pl.BlockSpec(memory_space=pltpu.VMEM),
        out_shape=jax.ShapeDtypeStruct((states, width), jnp.float32),
        scratch_shapes=[
            pltpu.VMEM((n_dep, states, k), got.dtype),
            pltpu.VMEM((n_dep, k, width), own.dtype),
            pltpu.SemaphoreType.DMA((n_dep + 1,)),
        ],
        compiler_params=params(),
        cost_estimate=cost(0.01),
    )(depth.reshape(1), got, own, *forward, *backward)


def make_local(n_low, n_up, n_dep):
    n_core = n_low // n_up
    others = range(1, n_up)
    same_core = [[(y * n_core + c) * n_dep + z for y in range(n_up) for z in range(n_dep)] for c in range(n_core)]

    def shifted(x, shift):
        return lax.ppermute(x, "upper", [((u + shift) % n_up, u) for u in range(n_up)])

    def low(y, c):
        return (y % n_up) * n_core + c

    def local(
        lower_vectors, upper_vectors, energy_lower, energy_upper, sym_lower, sym_upper, j_lower, j_upper
    ):
        lower_rows = lower_vectors[0]
        upper_rows = upper_vectors[0]
        rows, cols = lower_rows.shape
        width = upper_rows.shape[1]
        mine = energy_lower.shape[0]
        per_block = cols // mine
        unit = rows // 16
        main_rows = 12 * unit
        half = mine // 2
        me = lax.axis_index("upper")
        depth = lax.axis_index("depth")
        my_low = lax.axis_index("lower")
        my_y, my_core = my_low // n_core, my_low % n_core

        parity = sym_lower % 2
        sym_rule = sym_upper[None, :] - sym_lower[:, None] == (1 - 2 * parity)[:, None]
        j_rule = jnp.abs(j_upper[None, :] - j_lower[:, None]) <= 1
        allowed = jnp.logical_and(sym_rule, j_rule)
        frequency = energy_upper[None, :] - energy_lower[:, None]
        weight_upper = (2 * j_upper + 1).astype(jnp.float32)
        cubed = frequency * frequency * frequency

        crossed = []

        def cross(x, *others_first):
            if len(crossed) > 1:
                x = after(x, *crossed[-2], *others_first)
            crossed.append([shifted(x, s) for s in others])

        up = [(z, z + 1) for z in range(n_dep - 1)]
        down = [(z + 1, z) for z in range(n_dep - 1)]
        forward, backward = [], []

        def pass_on(held_up, held_down):
            i = len(forward)
            forward.append(lax.ppermute(held_up, "depth", up[i:]))
            backward.append(lax.ppermute(held_down, "depth", down[: n_dep - 1 - i]))

        first = lower_rows[main_rows : main_rows + 2 * unit]
        cross(first)
        later_rows = after(lower_rows, first)
        *turned, tail_rows = turn(later_rows, 2, unit, mine, n_dep)
        cross(after(turned[0], *crossed[0]))
        up_tail = after(upper_rows[main_rows + 2 * unit :], *crossed[0])
        pass_on(up_tail, up_tail)
        for i in range(1, n_dep - 1):
            pass_on(forward[-1], backward[-1])
        sorted_tail = lax.all_to_all(tail_rows, "depth", 0, 0)
        own = rows_product(after(later_rows, turned[0]), upper_rows, 0, 4 * unit, (), per_block, 2)
        cross(turned[1])
        so_far = [rows_product(g, upper_rows, main_rows, 2 * unit, (), per_block, 2) for g in crossed[0]]

        def reduced(i, got, *others_first):
            mine_of, *for_others = turned_products(me, my_core, own[i], [x[i] for x in so_far], got, upper_rows, n_core)
            total = mine_of
            for k, leaving in enumerate(for_others, 1):
                pairs = [(low(y, c), low(y, (c + k) % n_core)) for y in range(n_up) for c in range(n_core)]
                total = total + lax.ppermute(leaving, "lower", pairs)
            total = after(total, *others_first)
            by_owner = total.reshape(n_up * n_dep, half, width)
            return total, jnp.sum(lax.all_to_all(by_owner, OWNERS, 0, 0, axis_index_groups=same_core), axis=0)

        _, sum_a = reduced(0, crossed[1], sorted_tail)
        cross(sorted_tail, sum_a)
        last, sum_b = reduced(1, crossed[2], sum_a)
        main = jnp.concatenate([sum_a, sum_b], axis=0)

        terms = [tail_product(depth, after(g, last), up_tail, forward, backward) for g in crossed[3]]

        def term_for(y):
            block = jnp.zeros_like(terms[0])
            for s in others:
                block = jnp.where((me + s) % n_up == y % n_up, terms[s - 1], block)
            return block

        total = main
        for t in range(n_up):
            by_core = term_for(my_y + t).reshape(n_core, mine, width)
            for k in range(n_core):
                term = lax.dynamic_index_in_dim(by_core, (my_core + k) % n_core, 0, keepdims=False)
                if t or k:
                    pairs = [(low(y, c), low(y + t, (c + k) % n_core)) for y in range(n_up) for c in range(n_core)]
                    term = lax.ppermute(term, "lower", pairs)
                total = total + term
        value = cubed * (total * total) / weight_upper[None, :]
        return jnp.where(allowed, value, jnp.zeros_like(value))

    return local


def solution(mesh):
    return jax.shard_map(
        make_local(mesh.shape["lower"], mesh.shape["upper"], mesh.shape["depth"]),
        mesh=mesh,
        in_specs=(
            P("depth", "lower", "upper"),
            P("depth", "lower", "upper"),
            P(("lower", "depth")),
            P("upper"),
            P(("lower", "depth")),
            P("upper"),
            P(("lower", "depth")),
            P("upper"),
        ),
        out_specs=P(("lower", "depth"), "upper"),
        check_vma=False,
    )
```

```python
import jax
import jax.numpy as jnp
from jax import lax
from jax.experimental import pallas as pl
from jax.experimental.pallas import tpu as pltpu
from jax.sharding import PartitionSpec as P

OWNERS = ("lower", "depth")
VMEM_LIMIT = 16 * 1024 * 1024


def params():
    return pltpu.CompilerParams(vmem_limit_bytes=VMEM_LIMIT)


def cost(microseconds):
    return pl.CostEstimate(flops=0, bytes_accessed=int(microseconds * 3.0e6), transcendentals=0)


def dot(a, b):
    return jnp.dot(a, b, preferred_element_type=jnp.float32)


def after(x, *others):
    return lax.optimization_barrier((x,) + others)[0]


def in_hbm(x):
    return pltpu.with_memory_space_constraint(x, pltpu.HBM)


def whole(shape):
    return pl.BlockSpec(shape, lambda *_: (0,) * len(shape))


def turn(lower_rows, parts, unit, mine, n_dep):
    rows, cols = lower_rows.shape
    per_block = cols // mine
    kind = lower_rows.dtype
    block = 2 * unit
    mains = rows // block - 2

    def body(low, *outs):
        i = pl.program_id(0)
        flipped = low[...].astype(jnp.float32).T

        @pl.when(i < mains)
        def _():
            for out, part in zip(outs, split_states(flipped, per_block, parts)):
                out[...] = part.astype(kind)

        @pl.when(i == mains)
        def _():
            by_depth = flipped.reshape(per_block // n_dep, n_dep, mine, block)
            for z in range(n_dep):
                outs[-1][z] = by_depth[:, z].reshape(cols // n_dep, block).astype(kind)

    tail_shape = (n_dep, cols // n_dep, block)
    return pl.pallas_call(
        body,
        grid=(mains + 1,),
        in_specs=[pl.BlockSpec((block, cols), lambda i: (jnp.where(i < mains, i, i + 1), 0))],
        out_specs=[pl.BlockSpec((cols // parts, block), lambda i: (0, jnp.minimum(i, mains - 1)))] * parts
        + [whole(tail_shape)],
        out_shape=[jax.ShapeDtypeStruct((cols // parts, mains * block), kind)] * parts
        + [jax.ShapeDtypeStruct(tail_shape, kind)],
        compiler_params=params(),
        cost_estimate=cost(0.01),
    )(in_hbm(lower_rows))


def split_states(product, per_block, parts):
    states, width = product.shape
    by_owner = product.reshape(per_block, parts, states // per_block // parts, width)
    return [by_owner[:, i].reshape(states // parts, width) for i in range(parts)]


def rows_product(got, upper_rows, first, block, so_far, per_block, parts):
    k, states = got.shape
    width = upper_rows.shape[1]
    steps = k // block

    def body(low, up, *refs):
        outs, total = refs[-1 - parts : -1], refs[-1]
        i = pl.program_id(0)
        term = dot(low[...].T, up[...])

        @pl.when(i == 0)
        def _():
            total[...] = term

        @pl.when(i > 0)
        def _():
            total[...] += term

        @pl.when(i == steps - 1)
        def _():
            for j, part in enumerate(split_states(total[...], per_block, parts)):
                outs[j][...] = part + refs[j][...] if so_far else part

    shape = (states // parts, width)
    return pl.pallas_call(
        body,
        grid=(steps,),
        in_specs=[
            pl.BlockSpec((block, states), lambda i: (i, 0)),
            pl.BlockSpec((block, width), lambda i: (i + first // block, 0)),
        ]
        + [whole(shape)] * len(so_far),
        out_specs=[whole(shape)] * parts,
        out_shape=[jax.ShapeDtypeStruct(shape, jnp.float32)] * parts,
        scratch_shapes=[pltpu.VMEM((states, width), jnp.float32)],
        compiler_params=params(),
        cost_estimate=cost(0.01),
    )(got, in_hbm(upper_rows), *so_far)


def turned_products(me, core, own, so_far, got, upper_rows, n_core):
    n_up = 1 + len(got)
    states, k = got[0].shape
    width = upper_rows.shape[1]
    steps = 3
    block = k // steps
    share = states // n_core

    def body(me_at, core_at, mine, up, *refs):
        befores, lows_at = refs[: n_up - 1], refs[n_up - 1 : 2 * n_up - 2]
        outs = refs[2 * n_up - 2 : 2 * n_up - 2 + n_core]
        lows, ups, sems = refs[2 * n_up - 2 + n_core :]

        def start(source, target, sem):
            copy = pltpu.make_async_copy(source, target, sem)
            copy.start()
            return copy

        copies = []
        for j in range(steps):
            span = pl.ds(j * block, block)
            copies.append(
                [start(up.at[span], ups.at[j], sems.at[0, j])]
                + [start(low.at[:, span], lows.at[i, j], sems.at[i + 1, j]) for i, low in enumerate(lows_at)]
            )

        def put(slot, product):
            by_core = product.reshape(n_core, share, width)
            for c in range(n_core):
                for t, out in enumerate(outs):

                    @pl.when(lax.rem(core_at[0] + t, n_core) == c)
                    def _():
                        out[slot] = by_core[c]

        put(me_at[0], mine[...])
        totals = [before[...] for before in befores]
        for j, group in enumerate(copies):
            for copy in group:
                copy.wait()
            totals = [total + dot(lows[i, j], ups[j]) for i, total in enumerate(totals)]
        for i, total in enumerate(totals):
            put(lax.rem(me_at[0] + 1 + i, n_up), total)

    vmem, hbm = pl.BlockSpec(memory_space=pltpu.VMEM), pl.BlockSpec(memory_space=pltpu.HBM)
    return pl.pallas_call(
        body,
        in_specs=[pl.BlockSpec(memory_space=pltpu.SMEM)] * 2 + [vmem, hbm] + [vmem] * (n_up - 1) + [hbm] * (n_up - 1),
        out_specs=[vmem] * n_core,
        out_shape=[jax.ShapeDtypeStruct((n_up, share, width), jnp.float32)] * n_core,
        scratch_shapes=[
            pltpu.VMEM((n_up - 1, steps, states, block), got[0].dtype),
            pltpu.VMEM((steps, block, width), upper_rows.dtype),
            pltpu.SemaphoreType.DMA((n_up, steps)),
        ],
        compiler_params=params(),
        cost_estimate=cost(0.01),
    )(me.reshape(1), core.reshape(1), own, in_hbm(upper_rows), *so_far, *got)


def tail_product(depth, got, own, forward, backward):
    n_dep, states, k = got.shape
    width = own.shape[1]
    n = n_dep - 1

    def body(at, low, mid, *refs):
        out, lows, ups, sems = refs[2 * n :]
        z = at[0]
        of_low = pltpu.make_async_copy(low, lows, sems.at[n_dep])
        of_low.start()
        copies = [pltpu.make_async_copy(mid, ups.at[0], sems.at[0])]
        copies[0].start()
        for j in range(1, n_dep):
            down = pltpu.make_async_copy(refs[n + j - 1], ups.at[j], sems.at[j])
            round_ = pltpu.make_async_copy(refs[n - j], ups.at[j], sems.at[j])
            pl.when(z + j < n_dep)(down.start)
            pl.when(z + j >= n_dep)(round_.start)
            copies.append(down)
        of_low.wait()
        total = jnp.zeros((states, width), jnp.float32)
        for j, copy in enumerate(copies):
            copy.wait()
            total = total + dot(lows[lax.rem(z + j, n_dep)], ups[j])
        out[...] = total

    hbm = pl.BlockSpec(memory_space=pltpu.HBM)
    return pl.pallas_call(
        body,
        in_specs=[pl.BlockSpec(memory_space=pltpu.SMEM)] + [hbm] * (2 + 2 * n),
        out_specs=pl.BlockSpec(memory_space=pltpu.VMEM),
        out_shape=jax.ShapeDtypeStruct((states, width), jnp.float32),
        scratch_shapes=[
            pltpu.VMEM((n_dep, states, k), got.dtype),
            pltpu.VMEM((n_dep, k, width), own.dtype),
            pltpu.SemaphoreType.DMA((n_dep + 1,)),
        ],
        compiler_params=params(),
        cost_estimate=cost(0.01),
    )(depth.reshape(1), got, own, *forward, *backward)


def make_local(n_low, n_up, n_dep):
    n_core = n_low // n_up
    others = range(1, n_up)
    same_core = [[(y * n_core + c) * n_dep + z for y in range(n_up) for z in range(n_dep)] for c in range(n_core)]

    def shifted(x, shift):
        return lax.ppermute(x, "upper", [((u + shift) % n_up, u) for u in range(n_up)])

    def low(y, c):
        return (y % n_up) * n_core + c

    def local(
        lower_vectors, upper_vectors, energy_lower, energy_upper, sym_lower, sym_upper, j_lower, j_upper
    ):
        lower_rows = lower_vectors[0]
        upper_rows = upper_vectors[0]
        rows, cols = lower_rows.shape
        width = upper_rows.shape[1]
        mine = energy_lower.shape[0]
        per_block = cols // mine
        unit = rows // 16
        main_rows = 12 * unit
        half = mine // 2
        me = lax.axis_index("upper")
        depth = lax.axis_index("depth")
        my_low = lax.axis_index("lower")
        my_y, my_core = my_low // n_core, my_low % n_core

        parity = sym_lower % 2
        sym_rule = sym_upper[None, :] - sym_lower[:, None] == (1 - 2 * parity)[:, None]
        j_rule = jnp.abs(j_upper[None, :] - j_lower[:, None]) <= 1
        allowed = jnp.logical_and(sym_rule, j_rule)
        frequency = energy_upper[None, :] - energy_lower[:, None]
        weight_upper = (2 * j_upper + 1).astype(jnp.float32)
        cubed = frequency * frequency * frequency

        crossed = []

        def cross(x, *others_first):
            if len(crossed) > 1:
                x = after(x, *crossed[-2], *others_first)
            crossed.append([shifted(x, s) for s in others])

        up = [(z, z + 1) for z in range(n_dep - 1)]
        down = [(z + 1, z) for z in range(n_dep - 1)]
        forward, backward = [], []

        def pass_on(held_up, held_down):
            i = len(forward)
            forward.append(lax.ppermute(held_up, "depth", up[i:]))
            backward.append(lax.ppermute(held_down, "depth", down[: n_dep - 1 - i]))

        first = lower_rows[main_rows : main_rows + 2 * unit]
        cross(first)
        later_rows = after(lower_rows, first)
        *turned, tail_rows = turn(later_rows, 2, unit, mine, n_dep)
        cross(turned[0])
        up_tail = after(upper_rows[main_rows + 2 * unit :], *crossed[0])
        pass_on(up_tail, up_tail)
        for i in range(1, n_dep - 1):
            pass_on(forward[-1], backward[-1])
        sorted_tail = lax.all_to_all(tail_rows, "depth", 0, 0)
        own = rows_product(after(later_rows, turned[0]), upper_rows, 0, 4 * unit, (), per_block, 2)
        cross(turned[1])
        so_far = [rows_product(g, upper_rows, main_rows, 2 * unit, (), per_block, 2) for g in crossed[0]]

        def reduced(i, got, *others_first):
            mine_of, *for_others = turned_products(me, my_core, own[i], [x[i] for x in so_far], got, upper_rows, n_core)
            total = mine_of
            for k, leaving in enumerate(for_others, 1):
                pairs = [(low(y, c), low(y, (c + k) % n_core)) for y in range(n_up) for c in range(n_core)]
                total = total + lax.ppermute(leaving, "lower", pairs)
            total = after(total, *others_first)
            by_owner = total.reshape(n_up * n_dep, half, width)
            return total, jnp.sum(lax.all_to_all(by_owner, OWNERS, 0, 0, axis_index_groups=same_core), axis=0)

        _, sum_a = reduced(0, crossed[1], sorted_tail)
        cross(sorted_tail, sum_a)
        last, sum_b = reduced(1, crossed[2], sum_a)
        main = jnp.concatenate([sum_a, sum_b], axis=0)

        terms = [tail_product(depth, after(g, last), up_tail, forward, backward) for g in crossed[3]]

        def term_for(y):
            block = jnp.zeros_like(terms[0])
            for s in others:
                block = jnp.where((me + s) % n_up == y % n_up, terms[s - 1], block)
            return block

        total = main
        for t in range(n_up):
            by_core = term_for(my_y + t).reshape(n_core, mine, width)
            for k in range(n_core):
                term = lax.dynamic_index_in_dim(by_core, (my_core + k) % n_core, 0, keepdims=False)
                if t or k:
                    pairs = [(low(y, c), low(y + t, (c + k) % n_core)) for y in range(n_up) for c in range(n_core)]
                    term = lax.ppermute(term, "lower", pairs)
                total = total + term
        value = cubed * (total * total) / weight_upper[None, :]
        return jnp.where(allowed, value, jnp.zeros_like(value))

    return local


def solution(mesh):
    return jax.shard_map(
        make_local(mesh.shape["lower"], mesh.shape["upper"], mesh.shape["depth"]),
        mesh=mesh,
        in_specs=(
            P("depth", "lower", "upper"),
            P("depth", "lower", "upper"),
            P(("lower", "depth")),
            P("upper"),
            P(("lower", "depth")),
            P("upper"),
            P(("lower", "depth")),
            P("upper"),
        ),
        out_specs=P(("lower", "depth"), "upper"),
        check_vma=False,
    )
```

```python
import jax
import jax.numpy as jnp
from jax import lax
from jax.experimental import pallas as pl
from jax.experimental.pallas import tpu as pltpu
from jax.sharding import PartitionSpec as P

OWNERS = ("lower", "depth")
VMEM_LIMIT = 16 * 1024 * 1024


def params():
    return pltpu.CompilerParams(vmem_limit_bytes=VMEM_LIMIT)


def cost(microseconds):
    return pl.CostEstimate(flops=0, bytes_accessed=int(microseconds * 3.0e6), transcendentals=0)


def dot(a, b):
    return jnp.dot(a, b, preferred_element_type=jnp.float32)


def after(x, *others):
    return lax.optimization_barrier((x,) + others)[0]


def in_hbm(x):
    return pltpu.with_memory_space_constraint(x, pltpu.HBM)


def in_vmem(x):
    return pltpu.with_memory_space_constraint(x, pltpu.VMEM)


def whole(shape):
    return pl.BlockSpec(shape, lambda *_: (0,) * len(shape))


def turn(lower_rows, parts, unit, mine, n_dep):
    rows, cols = lower_rows.shape
    per_block = cols // mine
    kind = lower_rows.dtype
    block = 2 * unit
    mains = rows // block - 2

    def body(low, *outs):
        i = pl.program_id(0)
        flipped = low[...].astype(jnp.float32).T

        @pl.when(i < mains)
        def _():
            for out, part in zip(outs, split_states(flipped, per_block, parts)):
                out[...] = part.astype(kind)

        @pl.when(i == mains)
        def _():
            by_depth = flipped.reshape(per_block // n_dep, n_dep, mine, block)
            for z in range(n_dep):
                outs[-1][z] = by_depth[:, z].reshape(cols // n_dep, block).astype(kind)

    tail_shape = (n_dep, cols // n_dep, block)
    return pl.pallas_call(
        body,
        grid=(mains + 1,),
        in_specs=[pl.BlockSpec((block, cols), lambda i: (jnp.where(i < mains, i, i + 1), 0))],
        out_specs=[pl.BlockSpec((cols // parts, block), lambda i: (0, jnp.minimum(i, mains - 1)))] * parts
        + [whole(tail_shape)],
        out_shape=[jax.ShapeDtypeStruct((cols // parts, mains * block), kind)] * parts
        + [jax.ShapeDtypeStruct(tail_shape, kind)],
        compiler_params=params(),
        cost_estimate=cost(0.01),
    )(in_hbm(lower_rows))


def split_states(product, per_block, parts):
    states, width = product.shape
    by_owner = product.reshape(per_block, parts, states // per_block // parts, width)
    return [by_owner[:, i].reshape(states // parts, width) for i in range(parts)]


def rows_product(got, upper_rows, first, block, so_far, per_block, parts):
    k, states = got.shape
    width = upper_rows.shape[1]
    steps = k // block

    def body(low, up, *refs):
        outs, total = refs[-1 - parts : -1], refs[-1]
        i = pl.program_id(0)
        term = dot(low[...].T, up[...])

        @pl.when(i == 0)
        def _():
            total[...] = term

        @pl.when(i > 0)
        def _():
            total[...] += term

        @pl.when(i == steps - 1)
        def _():
            for j, part in enumerate(split_states(total[...], per_block, parts)):
                outs[j][...] = part + refs[j][...] if so_far else part

    shape = (states // parts, width)
    return pl.pallas_call(
        body,
        grid=(steps,),
        in_specs=[
            pl.BlockSpec((block, states), lambda i: (i, 0)),
            pl.BlockSpec((block, width), lambda i: (i + first // block, 0)),
        ]
        + [whole(shape)] * len(so_far),
        out_specs=[whole(shape)] * parts,
        out_shape=[jax.ShapeDtypeStruct(shape, jnp.float32)] * parts,
        scratch_shapes=[pltpu.VMEM((states, width), jnp.float32)],
        compiler_params=params(),
        cost_estimate=cost(0.01),
    )(got, in_hbm(upper_rows), *so_far)


def held_rows(upper_rows, k):
    width = upper_rows.shape[1]

    def body(up, out, sem):
        copy = pltpu.make_async_copy(up.at[pl.ds(0, k)], out, sem)
        copy.start()
        copy.wait()

    return pl.pallas_call(
        body,
        in_specs=[pl.BlockSpec(memory_space=pltpu.HBM)],
        out_specs=pl.BlockSpec(memory_space=pltpu.VMEM),
        out_shape=pltpu.VMEM((k, width), upper_rows.dtype),
        scratch_shapes=[pltpu.SemaphoreType.DMA],
        compiler_params=params(),
        cost_estimate=cost(0.01),
    )(in_hbm(upper_rows))


def turned_products(me, core, own, so_far, got, rows, n_core):
    n_up = 1 + len(got)
    states, k = got[0].shape
    width = rows.shape[1]
    steps = 3
    block = k // steps
    share = states // n_core

    def body(me_at, core_at, mine, up, *refs):
        befores, lows_at = refs[: n_up - 1], refs[n_up - 1 : 2 * n_up - 2]
        outs = refs[2 * n_up - 2 : 2 * n_up - 2 + n_core]
        lows, sems = refs[2 * n_up - 2 + n_core :]

        def start(source, target, sem):
            copy = pltpu.make_async_copy(source, target, sem)
            copy.start()
            return copy

        copies = []
        for j in range(steps):
            span = pl.ds(j * block, block)
            copies.append(
                [start(low.at[:, span], lows.at[i, j], sems.at[i, j]) for i, low in enumerate(lows_at)]
            )

        def put(slot, product):
            by_core = product.reshape(n_core, share, width)
            for c in range(n_core):
                for t, out in enumerate(outs):

                    @pl.when(lax.rem(core_at[0] + t, n_core) == c)
                    def _():
                        out[slot] = by_core[c]

        put(me_at[0], mine[...])
        totals = [before[...] for before in befores]
        for j, group in enumerate(copies):
            for copy in group:
                copy.wait()
            totals = [total + dot(lows[i, j], up[j * block : (j + 1) * block]) for i, total in enumerate(totals)]
        for i, total in enumerate(totals):
            put(lax.rem(me_at[0] + 1 + i, n_up), total)

    vmem, hbm = pl.BlockSpec(memory_space=pltpu.VMEM), pl.BlockSpec(memory_space=pltpu.HBM)
    return pl.pallas_call(
        body,
        in_specs=[pl.BlockSpec(memory_space=pltpu.SMEM)] * 2 + [vmem] * (n_up + 1) + [hbm] * (n_up - 1),
        out_specs=[vmem] * n_core,
        out_shape=[jax.ShapeDtypeStruct((n_up, share, width), jnp.float32)] * n_core,
        scratch_shapes=[
            pltpu.VMEM((n_up - 1, steps, states, block), got[0].dtype),
            pltpu.SemaphoreType.DMA((n_up - 1, steps)),
        ],
        compiler_params=params(),
        cost_estimate=cost(0.01),
    )(me.reshape(1), core.reshape(1), own, in_vmem(rows), *so_far, *got)


def tail_product(depth, got, own, forward, backward):
    n_dep, states, k = got.shape
    width = own.shape[1]
    n = n_dep - 1

    def body(at, low, mid, *refs):
        out, lows, ups, sems = refs[2 * n :]
        z = at[0]
        of_low = pltpu.make_async_copy(low, lows, sems.at[n_dep])
        of_low.start()
        copies = [pltpu.make_async_copy(mid, ups.at[0], sems.at[0])]
        copies[0].start()
        for j in range(1, n_dep):
            down = pltpu.make_async_copy(refs[n + j - 1], ups.at[j], sems.at[j])
            round_ = pltpu.make_async_copy(refs[n - j], ups.at[j], sems.at[j])
            pl.when(z + j < n_dep)(down.start)
            pl.when(z + j >= n_dep)(round_.start)
            copies.append(down)
        of_low.wait()
        total = jnp.zeros((states, width), jnp.float32)
        for j, copy in enumerate(copies):
            copy.wait()
            total = total + dot(lows[lax.rem(z + j, n_dep)], ups[j])
        out[...] = total

    hbm = pl.BlockSpec(memory_space=pltpu.HBM)
    return pl.pallas_call(
        body,
        in_specs=[pl.BlockSpec(memory_space=pltpu.SMEM)] + [hbm] * (2 + 2 * n),
        out_specs=pl.BlockSpec(memory_space=pltpu.VMEM),
        out_shape=jax.ShapeDtypeStruct((states, width), jnp.float32),
        scratch_shapes=[
            pltpu.VMEM((n_dep, states, k), got.dtype),
            pltpu.VMEM((n_dep, k, width), own.dtype),
            pltpu.SemaphoreType.DMA((n_dep + 1,)),
        ],
        compiler_params=params(),
        cost_estimate=cost(0.01),
    )(depth.reshape(1), got, own, *forward, *backward)


def make_local(n_low, n_up, n_dep):
    n_core = n_low // n_up
    others = range(1, n_up)
    same_core = [[(y * n_core + c) * n_dep + z for y in range(n_up) for z in range(n_dep)] for c in range(n_core)]

    def shifted(x, shift):
        return lax.ppermute(x, "upper", [((u + shift) % n_up, u) for u in range(n_up)])

    def low(y, c):
        return (y % n_up) * n_core + c

    def local(
        lower_vectors, upper_vectors, energy_lower, energy_upper, sym_lower, sym_upper, j_lower, j_upper
    ):
        lower_rows = lower_vectors[0]
        upper_rows = upper_vectors[0]
        rows, cols = lower_rows.shape
        width = upper_rows.shape[1]
        mine = energy_lower.shape[0]
        per_block = cols // mine
        unit = rows // 16
        main_rows = 12 * unit
        half = mine // 2
        me = lax.axis_index("upper")
        depth = lax.axis_index("depth")
        my_low = lax.axis_index("lower")
        my_y, my_core = my_low // n_core, my_low % n_core

        parity = sym_lower % 2
        sym_rule = sym_upper[None, :] - sym_lower[:, None] == (1 - 2 * parity)[:, None]
        j_rule = jnp.abs(j_upper[None, :] - j_lower[:, None]) <= 1
        allowed = jnp.logical_and(sym_rule, j_rule)
        frequency = energy_upper[None, :] - energy_lower[:, None]
        weight_upper = (2 * j_upper + 1).astype(jnp.float32)
        cubed = frequency * frequency * frequency

        crossed = []

        def cross(x, *others_first):
            if len(crossed) > 1:
                x = after(x, *crossed[-2], *others_first)
            crossed.append([shifted(x, s) for s in others])

        up = [(z, z + 1) for z in range(n_dep - 1)]
        down = [(z + 1, z) for z in range(n_dep - 1)]
        forward, backward = [], []

        def pass_on(held_up, held_down):
            i = len(forward)
            forward.append(lax.ppermute(held_up, "depth", up[i:]))
            backward.append(lax.ppermute(held_down, "depth", down[: n_dep - 1 - i]))

        first = lower_rows[main_rows : main_rows + 2 * unit]
        cross(first)
        later_rows = after(lower_rows, first)
        *turned, tail_rows = turn(later_rows, 2, unit, mine, n_dep)
        cross(turned[0])
        up_tail = after(upper_rows[main_rows + 2 * unit :], *crossed[0])
        pass_on(up_tail, up_tail)
        sorted_tail = lax.all_to_all(tail_rows, "depth", 0, 0)
        own = rows_product(after(later_rows, turned[0]), upper_rows, 0, 4 * unit, (), per_block, 2)
        cross(turned[1])
        so_far = [rows_product(g, upper_rows, main_rows, 2 * unit, (), per_block, 2) for g in crossed[0]]
        for i in range(1, n_dep - 1):
            held = (forward[-1], backward[-1])
            pass_on(*(after(held, *own, *so_far[0]) if i == 1 else held))

        def reduced(i, got, main_held, *others_first):
            mine_of, *for_others = turned_products(me, my_core, own[i], [x[i] for x in so_far], got, main_held, n_core)
            total = mine_of
            for k, leaving in enumerate(for_others, 1):
                pairs = [(low(y, c), low(y, (c + k) % n_core)) for y in range(n_up) for c in range(n_core)]
                total = total + lax.ppermute(leaving, "lower", pairs)
            total = after(total, *others_first)
            by_owner = total.reshape(n_up * n_dep, half, width)
            return total, jnp.sum(lax.all_to_all(by_owner, OWNERS, 0, 0, axis_index_groups=same_core), axis=0)

        _, sum_a = reduced(0, crossed[1], held_rows(after(upper_rows, *so_far[0]), main_rows), sorted_tail)
        cross(sorted_tail, sum_a)
        last, sum_b = reduced(1, crossed[2], held_rows(after(upper_rows, sum_a), main_rows), sum_a)
        main = jnp.concatenate([sum_a, sum_b], axis=0)

        terms = [tail_product(depth, after(g, last), up_tail, forward, backward) for g in crossed[3]]

        def term_for(y):
            block = jnp.zeros_like(terms[0])
            for s in others:
                block = jnp.where((me + s) % n_up == y % n_up, terms[s - 1], block)
            return block

        total = main
        for t in range(n_up):
            by_core = term_for(my_y + t).reshape(n_core, mine, width)
            for k in range(n_core):
                term = lax.dynamic_index_in_dim(by_core, (my_core + k) % n_core, 0, keepdims=False)
                if t or k:
                    pairs = [(low(y, c), low(y + t, (c + k) % n_core)) for y in range(n_up) for c in range(n_core)]
                    term = lax.ppermute(term, "lower", pairs)
                total = total + term
        value = cubed * (total * total) / weight_upper[None, :]
        return jnp.where(allowed, value, jnp.zeros_like(value))

    return local


def solution(mesh):
    return jax.shard_map(
        make_local(mesh.shape["lower"], mesh.shape["upper"], mesh.shape["depth"]),
        mesh=mesh,
        in_specs=(
            P("depth", "lower", "upper"),
            P("depth", "lower", "upper"),
            P(("lower", "depth")),
            P("upper"),
            P(("lower", "depth")),
            P("upper"),
            P(("lower", "depth")),
            P("upper"),
        ),
        out_specs=P(("lower", "depth"), "upper"),
        check_vma=False,
    )
```

```python
import jax
import jax.numpy as jnp
from jax import lax
from jax.experimental import pallas as pl
from jax.experimental.pallas import tpu as pltpu
from jax.sharding import PartitionSpec as P

OWNERS = ("lower", "depth")
VMEM_LIMIT = 16 * 1024 * 1024


def params():
    return pltpu.CompilerParams(vmem_limit_bytes=VMEM_LIMIT)


def cost(microseconds):
    return pl.CostEstimate(flops=0, bytes_accessed=int(microseconds * 3.0e6), transcendentals=0)


def dot(a, b):
    return jnp.dot(a, b, preferred_element_type=jnp.float32)


def after(x, *others):
    return lax.optimization_barrier((x,) + others)[0]


def in_hbm(x):
    return pltpu.with_memory_space_constraint(x, pltpu.HBM)


def in_vmem(x):
    return pltpu.with_memory_space_constraint(x, pltpu.VMEM)


def whole(shape):
    return pl.BlockSpec(shape, lambda *_: (0,) * len(shape))


def turn(lower_rows, n_tail, n_main, parts, mine, n_dep):
    rows, cols = lower_rows.shape
    per_block = cols // mine
    kind = lower_rows.dtype
    steps = 6
    block = n_main // steps
    skipped = (rows - n_main) // block

    def body(low, low_tail, *outs):
        flipped = low[...].astype(jnp.float32).T
        for out, part in zip(outs, split_states(flipped, per_block, parts)):
            out[...] = part.astype(kind)

        @pl.when(pl.program_id(0) == steps - 1)
        def _():
            by_depth = low_tail[...].astype(jnp.float32).T.reshape(per_block // n_dep, n_dep, mine, n_tail)
            for z in range(n_dep):
                outs[-1][z] = by_depth[:, z].reshape(cols // n_dep, n_tail).astype(kind)

    tail_shape = (n_dep, cols // n_dep, n_tail)
    return pl.pallas_call(
        body,
        grid=(steps,),
        in_specs=[
            pl.BlockSpec((block, cols), lambda i: (i + skipped, 0)),
            pl.BlockSpec((n_tail, cols), lambda i: (0, 0)),
        ],
        out_specs=[pl.BlockSpec((cols // parts, block), lambda i: (0, i))] * parts + [whole(tail_shape)],
        out_shape=[jax.ShapeDtypeStruct((cols // parts, n_main), kind)] * parts
        + [jax.ShapeDtypeStruct(tail_shape, kind)],
        compiler_params=params(),
        cost_estimate=cost(0.01),
    )(in_hbm(lower_rows), in_hbm(lower_rows))


def split_states(product, per_block, parts):
    states, width = product.shape
    by_owner = product.reshape(per_block, parts, states // per_block // parts, width)
    return [by_owner[:, i].reshape(states // parts, width) for i in range(parts)]


def rows_product(got, upper_rows, first, block, so_far, per_block, parts):
    k, states = got.shape
    width = upper_rows.shape[1]
    steps = k // block

    def body(low, up, *refs):
        outs, total = refs[-1 - parts : -1], refs[-1]
        i = pl.program_id(0)
        term = dot(low[...].T, up[...])

        @pl.when(i == 0)
        def _():
            total[...] = term

        @pl.when(i > 0)
        def _():
            total[...] += term

        @pl.when(i == steps - 1)
        def _():
            for j, part in enumerate(split_states(total[...], per_block, parts)):
                outs[j][...] = part + refs[j][...] if so_far else part

    shape = (states // parts, width)
    return pl.pallas_call(
        body,
        grid=(steps,),
        in_specs=[
            pl.BlockSpec((block, states), lambda i: (i, 0)),
            pl.BlockSpec((block, width), lambda i: (i + first // block, 0)),
        ]
        + [whole(shape)] * len(so_far),
        out_specs=[whole(shape)] * parts,
        out_shape=[jax.ShapeDtypeStruct(shape, jnp.float32)] * parts,
        scratch_shapes=[pltpu.VMEM((states, width), jnp.float32)],
        compiler_params=params(),
        cost_estimate=cost(0.01),
    )(got, in_hbm(upper_rows), *so_far)


def held_rows(rows, first, k):
    width = rows.shape[1]

    def body(up, out, sem):
        copy = pltpu.make_async_copy(up.at[pl.ds(first, k)], out, sem)
        copy.start()
        copy.wait()

    return pl.pallas_call(
        body,
        in_specs=[pl.BlockSpec(memory_space=pltpu.HBM)],
        out_specs=pl.BlockSpec(memory_space=pltpu.VMEM),
        out_shape=pltpu.VMEM((k, width), rows.dtype),
        scratch_shapes=[pltpu.SemaphoreType.DMA],
        compiler_params=params(),
        cost_estimate=cost(0.01),
    )(in_hbm(rows))


def turned_products(me, core, own, so_far, got, rows, n_core):
    n_up = 1 + len(got)
    states, k = got[0].shape
    width = rows.shape[1]
    steps = 3
    block = k // steps
    share = states // n_core

    def body(me_at, core_at, mine, up, *refs):
        befores, lows_at = refs[: n_up - 1], refs[n_up - 1 : 2 * n_up - 2]
        outs = refs[2 * n_up - 2 : 2 * n_up - 2 + n_core]
        lows, sems = refs[2 * n_up - 2 + n_core :]

        def start(source, target, sem):
            copy = pltpu.make_async_copy(source, target, sem)
            copy.start()
            return copy

        copies = []
        for j in range(steps):
            span = pl.ds(j * block, block)
            copies.append(
                [start(low.at[:, span], lows.at[i, j], sems.at[i, j]) for i, low in enumerate(lows_at)]
            )

        def put(slot, product):
            by_core = product.reshape(n_core, share, width)
            for c in range(n_core):
                for t, out in enumerate(outs):

                    @pl.when(lax.rem(core_at[0] + t, n_core) == c)
                    def _():
                        out[slot] = by_core[c]

        put(me_at[0], mine[...])
        totals = [before[...] for before in befores]
        for j, group in enumerate(copies):
            for copy in group:
                copy.wait()
            totals = [total + dot(lows[i, j], up[j * block : (j + 1) * block]) for i, total in enumerate(totals)]
        for i, total in enumerate(totals):
            put(lax.rem(me_at[0] + 1 + i, n_up), total)

    vmem, hbm = pl.BlockSpec(memory_space=pltpu.VMEM), pl.BlockSpec(memory_space=pltpu.HBM)
    return pl.pallas_call(
        body,
        in_specs=[pl.BlockSpec(memory_space=pltpu.SMEM)] * 2 + [vmem] * (n_up + 1) + [hbm] * (n_up - 1),
        out_specs=[vmem] * n_core,
        out_shape=[jax.ShapeDtypeStruct((n_up, share, width), jnp.float32)] * n_core,
        scratch_shapes=[
            pltpu.VMEM((n_up - 1, steps, states, block), got[0].dtype),
            pltpu.SemaphoreType.DMA((n_up - 1, steps)),
        ],
        compiler_params=params(),
        cost_estimate=cost(0.01),
    )(me.reshape(1), core.reshape(1), own, in_vmem(rows), *so_far, *got)


def tail_product(depth, got, own, forward, backward):
    n_dep, states, k = got.shape
    width = own.shape[1]
    n = n_dep - 1

    def body(at, low, mid, *refs):
        out, lows, ups, sems = refs[2 * n :]
        z = at[0]
        of_low = pltpu.make_async_copy(low, lows, sems.at[n_dep])
        of_low.start()
        copies = [pltpu.make_async_copy(mid, ups.at[0], sems.at[0])]
        copies[0].start()
        for j in range(1, n_dep):
            down = pltpu.make_async_copy(refs[n + j - 1], ups.at[j], sems.at[j])
            round_ = pltpu.make_async_copy(refs[n - j], ups.at[j], sems.at[j])
            pl.when(z + j < n_dep)(down.start)
            pl.when(z + j >= n_dep)(round_.start)
            copies.append(down)
        of_low.wait()
        total = jnp.zeros((states, width), jnp.float32)
        for j, copy in enumerate(copies):
            copy.wait()
            total = total + dot(lows[lax.rem(z + j, n_dep)], ups[j])
        out[...] = total

    hbm = pl.BlockSpec(memory_space=pltpu.HBM)
    return pl.pallas_call(
        body,
        in_specs=[pl.BlockSpec(memory_space=pltpu.SMEM)] + [hbm] * (2 + 2 * n),
        out_specs=pl.BlockSpec(memory_space=pltpu.VMEM),
        out_shape=jax.ShapeDtypeStruct((states, width), jnp.float32),
        scratch_shapes=[
            pltpu.VMEM((n_dep, states, k), got.dtype),
            pltpu.VMEM((n_dep, k, width), own.dtype),
            pltpu.SemaphoreType.DMA((n_dep + 1,)),
        ],
        compiler_params=params(),
        cost_estimate=cost(0.01),
    )(depth.reshape(1), got, own, *forward, *backward)


def make_local(n_low, n_up, n_dep):
    n_core = n_low // n_up
    others = range(1, n_up)
    same_core = [[(y * n_core + c) * n_dep + z for y in range(n_up) for z in range(n_dep)] for c in range(n_core)]

    def shifted(x, shift):
        return lax.ppermute(x, "upper", [((u + shift) % n_up, u) for u in range(n_up)])

    def low(y, c):
        return (y % n_up) * n_core + c

    def local(
        lower_vectors, upper_vectors, energy_lower, energy_upper, sym_lower, sym_upper, j_lower, j_upper
    ):
        lower_rows = lower_vectors[0]
        upper_rows = upper_vectors[0]
        rows, cols = lower_rows.shape
        width = upper_rows.shape[1]
        mine = energy_lower.shape[0]
        per_block = cols // mine
        unit = rows // 64
        n_tail, n_head, n_main = 9 * unit, 7 * unit, 48 * unit
        half = mine // 2
        me = lax.axis_index("upper")
        depth = lax.axis_index("depth")
        my_low = lax.axis_index("lower")
        my_y, my_core = my_low // n_core, my_low % n_core

        parity = sym_lower % 2
        sym_rule = sym_upper[None, :] - sym_lower[:, None] == (1 - 2 * parity)[:, None]
        j_rule = jnp.abs(j_upper[None, :] - j_lower[:, None]) <= 1
        allowed = jnp.logical_and(sym_rule, j_rule)
        frequency = energy_upper[None, :] - energy_lower[:, None]
        weight_upper = (2 * j_upper + 1).astype(jnp.float32)
        cubed = frequency * frequency * frequency

        crossed = []

        def cross(x, *others_first):
            if len(crossed) > 1:
                x = after(x, *crossed[-2], *others_first)
            crossed.append([shifted(x, s) for s in others])

        up = [(z, z + 1) for z in range(n_dep - 1)]
        down = [(z + 1, z) for z in range(n_dep - 1)]
        forward, backward = [], []

        def pass_on(held_up, held_down):
            i = len(forward)
            forward.append(lax.ppermute(held_up, "depth", up[i:]))
            backward.append(lax.ppermute(held_down, "depth", down[: n_dep - 1 - i]))

        first = lower_rows[n_tail : n_tail + n_head]
        cross(first)
        later_rows = after(lower_rows, first)
        *turned, tail_rows = turn(later_rows, n_tail, n_main, 2, mine, n_dep)
        cross(turned[0])
        up_tail = after(upper_rows[:n_tail], *crossed[0])
        pass_on(up_tail, up_tail)
        sorted_tail = lax.all_to_all(tail_rows, "depth", 0, 0)
        own = rows_product(after(later_rows, turned[0]), upper_rows, 0, rows // 4, (), per_block, 2)
        cross(turned[1])
        head_rows = upper_rows[n_tail : n_tail + n_head]
        so_far = [rows_product(g, head_rows, 0, n_head, (), per_block, 2) for g in crossed[0]]
        for i in range(1, n_dep - 1):
            held = (forward[-1], backward[-1])
            pass_on(*(after(held, *own, *so_far[0]) if i == 1 else held))

        def reduced(i, got, main_held, *others_first):
            mine_of, *for_others = turned_products(me, my_core, own[i], [x[i] for x in so_far], got, main_held, n_core)
            total = mine_of
            for k, leaving in enumerate(for_others, 1):
                pairs = [(low(y, c), low(y, (c + k) % n_core)) for y in range(n_up) for c in range(n_core)]
                total = total + lax.ppermute(leaving, "lower", pairs)
            total = after(total, *others_first)
            by_owner = total.reshape(n_up * n_dep, half, width)
            return total, lax.all_to_all(by_owner, OWNERS, 0, 0, axis_index_groups=same_core)

        held_a = held_rows(after(upper_rows, *so_far[0]), rows - n_main, n_main)
        sent_a, from_a = reduced(0, crossed[1], held_a, sorted_tail)
        sum_a = jnp.sum(from_a, axis=0)
        held_b = held_rows(after(upper_rows, sum_a), rows - n_main, n_main)
        cross(sorted_tail, from_a)
        last, from_b = reduced(1, crossed[2], held_b, sum_a)
        sum_b = jnp.sum(from_b, axis=0)
        main = jnp.concatenate([sum_a, sum_b], axis=0)

        terms = [tail_product(depth, after(g, last), up_tail, forward, backward) for g in crossed[3]]

        def term_for(y):
            block = jnp.zeros_like(terms[0])
            for s in others:
                block = jnp.where((me + s) % n_up == y % n_up, terms[s - 1], block)
            return block

        total = main
        for t in reversed(range(n_up)):
            by_core = term_for(my_y + t).reshape(n_core, mine, width)
            for k in reversed(range(n_core)):
                term = lax.dynamic_index_in_dim(by_core, (my_core + k) % n_core, 0, keepdims=False)
                if t or k:
                    pairs = [(low(y, c), low(y + t, (c + k) % n_core)) for y in range(n_up) for c in range(n_core)]
                    term = lax.ppermute(term, "lower", pairs)
                total = total + term
        value = cubed * (total * total) / weight_upper[None, :]
        return jnp.where(allowed, value, jnp.zeros_like(value))

    return local


def solution(mesh):
    return jax.shard_map(
        make_local(mesh.shape["lower"], mesh.shape["upper"], mesh.shape["depth"]),
        mesh=mesh,
        in_specs=(
            P("depth", "lower", "upper"),
            P("depth", "lower", "upper"),
            P(("lower", "depth")),
            P("upper"),
            P(("lower", "depth")),
            P("upper"),
            P(("lower", "depth")),
            P("upper"),
        ),
        out_specs=P(("lower", "depth"), "upper"),
        check_vma=False,
    )
```

```python
import jax
import jax.numpy as jnp
from jax import lax
from jax.experimental import pallas as pl
from jax.experimental.pallas import tpu as pltpu
from jax.sharding import PartitionSpec as P

OWNERS = ("lower", "depth")
VMEM_LIMIT = 16 * 1024 * 1024


def params():
    return pltpu.CompilerParams(vmem_limit_bytes=VMEM_LIMIT)


def cost():
    return pl.CostEstimate(flops=0, bytes_accessed=30000, transcendentals=0)


def dot(a, b):
    return jnp.dot(a, b, preferred_element_type=jnp.float32)


def after(x, *others):
    return lax.optimization_barrier((x,) + others)[0]


def in_hbm(x):
    return pltpu.with_memory_space_constraint(x, pltpu.HBM)


def in_vmem(x):
    return pltpu.with_memory_space_constraint(x, pltpu.VMEM)


def whole(shape):
    return pl.BlockSpec(shape, lambda *_: (0,) * len(shape))


def turn(lower_rows, n_tail, n_main, parts, mine, n_dep):
    rows, cols = lower_rows.shape
    per_block = cols // mine
    kind = lower_rows.dtype
    steps = 6
    block = n_main // steps
    skipped = (rows - n_main) // block

    def body(low, low_tail, *outs):
        flipped = low[...].astype(jnp.float32).T
        for out, part in zip(outs, split_states(flipped, per_block, parts)):
            out[...] = part.astype(kind)

        @pl.when(pl.program_id(0) == steps - 1)
        def _():
            by_depth = low_tail[...].astype(jnp.float32).T.reshape(per_block // n_dep, n_dep, mine, n_tail)
            for z in range(n_dep):
                outs[-1][z] = by_depth[:, z].reshape(cols // n_dep, n_tail).astype(kind)

    tail_shape = (n_dep, cols // n_dep, n_tail)
    return pl.pallas_call(
        body,
        grid=(steps,),
        in_specs=[
            pl.BlockSpec((block, cols), lambda i: (i + skipped, 0)),
            pl.BlockSpec((n_tail, cols), lambda i: (0, 0)),
        ],
        out_specs=[pl.BlockSpec((cols // parts, block), lambda i: (0, i))] * parts + [whole(tail_shape)],
        out_shape=[jax.ShapeDtypeStruct((cols // parts, n_main), kind)] * parts
        + [jax.ShapeDtypeStruct(tail_shape, kind)],
        compiler_params=params(),
        cost_estimate=cost(),
    )(in_hbm(lower_rows), in_hbm(lower_rows))


def split_states(product, per_block, parts):
    states, width = product.shape
    by_owner = product.reshape(per_block, parts, states // per_block // parts, width)
    return [by_owner[:, i].reshape(states // parts, width) for i in range(parts)]


def rows_product(got, upper_rows, first, block, so_far, per_block, parts):
    k, states = got.shape
    width = upper_rows.shape[1]
    steps = k // block

    def body(low, up, *refs):
        outs, total = refs[-1 - parts : -1], refs[-1]
        i = pl.program_id(0)
        term = dot(low[...].T, up[...])

        @pl.when(i == 0)
        def _():
            total[...] = term

        @pl.when(i > 0)
        def _():
            total[...] += term

        @pl.when(i == steps - 1)
        def _():
            for j, part in enumerate(split_states(total[...], per_block, parts)):
                outs[j][...] = part + refs[j][...] if so_far else part

    shape = (states // parts, width)
    return pl.pallas_call(
        body,
        grid=(steps,),
        in_specs=[
            pl.BlockSpec((block, states), lambda i: (i, 0)),
            pl.BlockSpec((block, width), lambda i: (i + first // block, 0)),
        ]
        + [whole(shape)] * len(so_far),
        out_specs=[whole(shape)] * parts,
        out_shape=[jax.ShapeDtypeStruct(shape, jnp.float32)] * parts,
        scratch_shapes=[pltpu.VMEM((states, width), jnp.float32)],
        compiler_params=params(),
        cost_estimate=cost(),
    )(got, in_hbm(upper_rows), *so_far)


def held_rows(rows, first, k):
    width = rows.shape[1]

    def body(up, out, sem):
        copy = pltpu.make_async_copy(up.at[pl.ds(first, k)], out, sem)
        copy.start()
        copy.wait()

    return pl.pallas_call(
        body,
        in_specs=[pl.BlockSpec(memory_space=pltpu.HBM)],
        out_specs=pl.BlockSpec(memory_space=pltpu.VMEM),
        out_shape=pltpu.VMEM((k, width), rows.dtype),
        scratch_shapes=[pltpu.SemaphoreType.DMA],
        compiler_params=params(),
        cost_estimate=cost(),
    )(in_hbm(rows))


def turned_products(me, core, own, so_far, got, rows, n_core):
    n_up = 1 + len(got)
    states, k = got[0].shape
    width = rows.shape[1]
    steps = 1
    block = k // steps
    share = states // n_core

    def body(me_at, core_at, mine, up, *refs):
        befores, lows_at = refs[: n_up - 1], refs[n_up - 1 : 2 * n_up - 2]
        outs = refs[2 * n_up - 2 : 2 * n_up - 2 + n_core]
        lows, sems = refs[2 * n_up - 2 + n_core :]

        def start(source, target, sem):
            copy = pltpu.make_async_copy(source, target, sem)
            copy.start()
            return copy

        copies = []
        for j in range(steps):
            span = pl.ds(j * block, block)
            copies.append(
                [start(low.at[:, span], lows.at[i, j], sems.at[i, j]) for i, low in enumerate(lows_at)]
            )

        def put(slot, product):
            by_core = product.reshape(n_core, share, width)
            for c in range(n_core):
                for t, out in enumerate(outs):

                    @pl.when(lax.rem(core_at[0] + t, n_core) == c)
                    def _():
                        out[slot] = by_core[c]

        put(me_at[0], mine[...])
        totals = [before[...] for before in befores]
        for j, group in enumerate(copies):
            for copy in group:
                copy.wait()
            totals = [total + dot(lows[i, j], up[j * block : (j + 1) * block]) for i, total in enumerate(totals)]
        for i, total in enumerate(totals):
            put(lax.rem(me_at[0] + 1 + i, n_up), total)

    vmem, hbm = pl.BlockSpec(memory_space=pltpu.VMEM), pl.BlockSpec(memory_space=pltpu.HBM)
    return pl.pallas_call(
        body,
        in_specs=[pl.BlockSpec(memory_space=pltpu.SMEM)] * 2 + [vmem] * (n_up + 1) + [hbm] * (n_up - 1),
        out_specs=[vmem] * n_core,
        out_shape=[jax.ShapeDtypeStruct((n_up, share, width), jnp.float32)] * n_core,
        scratch_shapes=[
            pltpu.VMEM((n_up - 1, steps, states, block), got[0].dtype),
            pltpu.SemaphoreType.DMA((n_up - 1, steps)),
        ],
        compiler_params=params(),
        cost_estimate=cost(),
    )(me.reshape(1), core.reshape(1), own, in_vmem(rows), *so_far, *got)


def tail_product(depth, got, own, forward, backward):
    n_dep, states, k = got.shape
    width = own.shape[1]
    n = n_dep - 1

    def body(at, low, mid, *refs):
        out, lows, ups, sems = refs[2 * n :]
        z = at[0]
        of_low = pltpu.make_async_copy(low, lows, sems.at[n_dep])
        of_low.start()
        copies = [pltpu.make_async_copy(mid, ups.at[0], sems.at[0])]
        copies[0].start()
        for j in range(1, n_dep):
            down = pltpu.make_async_copy(refs[n + j - 1], ups.at[j], sems.at[j])
            round_ = pltpu.make_async_copy(refs[n - j], ups.at[j], sems.at[j])
            pl.when(z + j < n_dep)(down.start)
            pl.when(z + j >= n_dep)(round_.start)
            copies.append(down)
        of_low.wait()
        total = jnp.zeros((states, width), jnp.float32)
        for j, copy in enumerate(copies):
            copy.wait()
            total = total + dot(lows[lax.rem(z + j, n_dep)], ups[j])
        out[...] = total

    hbm = pl.BlockSpec(memory_space=pltpu.HBM)
    return pl.pallas_call(
        body,
        in_specs=[pl.BlockSpec(memory_space=pltpu.SMEM)] + [hbm] * (2 + 2 * n),
        out_specs=pl.BlockSpec(memory_space=pltpu.VMEM),
        out_shape=jax.ShapeDtypeStruct((states, width), jnp.float32),
        scratch_shapes=[
            pltpu.VMEM((n_dep, states, k), got.dtype),
            pltpu.VMEM((n_dep, k, width), own.dtype),
            pltpu.SemaphoreType.DMA((n_dep + 1,)),
        ],
        compiler_params=params(),
        cost_estimate=cost(),
    )(depth.reshape(1), got, own, *forward, *backward)


def make_local(n_low, n_up, n_dep):
    n_core = n_low // n_up
    others = range(1, n_up)
    same_core = [[(y * n_core + c) * n_dep + z for y in range(n_up) for z in range(n_dep)] for c in range(n_core)]

    def shifted(x, shift):
        return lax.ppermute(x, "upper", [((u + shift) % n_up, u) for u in range(n_up)])

    def low(y, c):
        return (y % n_up) * n_core + c

    def local(
        lower_vectors, upper_vectors, energy_lower, energy_upper, sym_lower, sym_upper, j_lower, j_upper
    ):
        lower_rows = lower_vectors[0]
        upper_rows = upper_vectors[0]
        rows, cols = lower_rows.shape
        width = upper_rows.shape[1]
        mine = energy_lower.shape[0]
        per_block = cols // mine
        unit = rows // 64
        n_tail, n_head, n_main = 9 * unit, 7 * unit, 48 * unit
        half = mine // 2
        me = lax.axis_index("upper")
        depth = lax.axis_index("depth")
        my_low = lax.axis_index("lower")
        my_y, my_core = my_low // n_core, my_low % n_core

        parity = sym_lower % 2
        sym_rule = sym_upper[None, :] - sym_lower[:, None] == (1 - 2 * parity)[:, None]
        j_rule = jnp.abs(j_upper[None, :] - j_lower[:, None]) <= 1
        allowed = jnp.logical_and(sym_rule, j_rule)
        frequency = energy_upper[None, :] - energy_lower[:, None]
        weight_upper = (2 * j_upper + 1).astype(jnp.float32)
        cubed = frequency * frequency * frequency

        crossed = []

        def cross(x, *others_first):
            if len(crossed) > 1:
                x = after(x, *crossed[-2], *others_first)
            crossed.append([shifted(x, s) for s in others])

        up = [(z, z + 1) for z in range(n_dep - 1)]
        down = [(z + 1, z) for z in range(n_dep - 1)]
        forward, backward = [], []

        def pass_on(held_up, held_down):
            i = len(forward)
            forward.append(lax.ppermute(held_up, "depth", up[i:]))
            backward.append(lax.ppermute(held_down, "depth", down[: n_dep - 1 - i]))

        first = lower_rows[n_tail : n_tail + n_head]
        cross(first)
        later_rows = after(lower_rows, first)
        *turned, tail_rows = turn(later_rows, n_tail, n_main, 2, mine, n_dep)
        cross(turned[0])
        up_tail = after(upper_rows[:n_tail], *crossed[0])
        pass_on(up_tail, up_tail)
        sorted_tail = lax.all_to_all(tail_rows, "depth", 0, 0)
        own = rows_product(after(later_rows, turned[0]), upper_rows, 0, rows // 4, (), per_block, 2)
        cross(turned[1])
        head_rows = upper_rows[n_tail : n_tail + n_head]
        so_far = [rows_product(g, head_rows, 0, n_head, (), per_block, 2) for g in crossed[0]]
        for i in range(1, n_dep - 1):
            held = (forward[-1], backward[-1])
            pass_on(*(after(held, *own, *so_far[0]) if i == 1 else held))

        def reduced(i, got, main_held, *others_first):
            mine_of, *for_others = turned_products(me, my_core, own[i], [x[i] for x in so_far], got, main_held, n_core)
            total = mine_of
            for k, leaving in enumerate(for_others, 1):
                pairs = [(low(y, c), low(y, (c + k) % n_core)) for y in range(n_up) for c in range(n_core)]
                total = total + lax.ppermute(leaving, "lower", pairs)
            total = after(total, *others_first)
            by_owner = total.reshape(n_up * n_dep, half, width)
            return total, lax.all_to_all(by_owner, OWNERS, 0, 0, axis_index_groups=same_core)

        held_a = held_rows(after(upper_rows, *so_far[0]), rows - n_main, n_main)
        sent_a, from_a = reduced(0, crossed[1], held_a, sorted_tail)
        held_b = held_rows(after(upper_rows, sent_a), rows - n_main, n_main)
        cross(sorted_tail, from_a)
        last, from_b = reduced(1, crossed[2], held_b, from_a)
        sum_a, sum_b = jnp.sum(from_a, axis=0), jnp.sum(from_b, axis=0)
        main = jnp.concatenate([sum_a, sum_b], axis=0)

        terms = [tail_product(depth, after(g, last), up_tail, forward, backward) for g in crossed[3]]

        def term_for(y):
            block = jnp.zeros_like(terms[0])
            for s in others:
                block = jnp.where((me + s) % n_up == y % n_up, terms[s - 1], block)
            return block

        total = main
        for t in reversed(range(n_up)):
            by_core = term_for(my_y + t).reshape(n_core, mine, width)
            for k in reversed(range(n_core)):
                term = lax.dynamic_index_in_dim(by_core, (my_core + k) % n_core, 0, keepdims=False)
                if t or k:
                    pairs = [(low(y, c), low(y + t, (c + k) % n_core)) for y in range(n_up) for c in range(n_core)]
                    term = lax.ppermute(term, "lower", pairs)
                total = total + term
        value = cubed * (total * total) / weight_upper[None, :]
        return jnp.where(allowed, value, jnp.zeros_like(value))

    return local


def solution(mesh):
    return jax.shard_map(
        make_local(mesh.shape["lower"], mesh.shape["upper"], mesh.shape["depth"]),
        mesh=mesh,
        in_specs=(
            P("depth", "lower", "upper"),
            P("depth", "lower", "upper"),
            P(("lower", "depth")),
            P("upper"),
            P(("lower", "depth")),
            P("upper"),
            P(("lower", "depth")),
            P("upper"),
        ),
        out_specs=P(("lower", "depth"), "upper"),
        check_vma=False,
    )
```

```python
import jax
import jax.numpy as jnp
from jax import lax
from jax.experimental import pallas as pl
from jax.experimental.pallas import tpu as pltpu
from jax.sharding import PartitionSpec as P

OWNERS = ("lower", "depth")
VMEM_LIMIT = 16 * 1024 * 1024


def params():
    return pltpu.CompilerParams(vmem_limit_bytes=VMEM_LIMIT)


def cost():
    return pl.CostEstimate(flops=0, bytes_accessed=30000, transcendentals=0)


def dot(a, b):
    return jnp.dot(a, b, preferred_element_type=jnp.float32)


def after(x, *others):
    return lax.optimization_barrier((x,) + others)[0]


def in_hbm(x):
    return pltpu.with_memory_space_constraint(x, pltpu.HBM)


def in_vmem(x):
    return pltpu.with_memory_space_constraint(x, pltpu.VMEM)


def whole(shape):
    return pl.BlockSpec(shape, lambda *_: (0,) * len(shape))


def turn(lower_rows, n_tail, n_main, parts, mine, n_dep):
    rows, cols = lower_rows.shape
    per_block = cols // mine
    kind = lower_rows.dtype
    steps = 6
    block = n_main // steps
    skipped = (rows - n_main) // block

    def body(low, low_tail, *outs):
        flipped = low[...].astype(jnp.float32).T
        for out, part in zip(outs, split_states(flipped, per_block, parts)):
            out[...] = part.astype(kind)

        @pl.when(pl.program_id(0) == steps - 1)
        def _():
            by_depth = low_tail[...].astype(jnp.float32).T.reshape(per_block // n_dep, n_dep, mine, n_tail)
            for z in range(n_dep):
                outs[-1][z] = by_depth[:, z].reshape(cols // n_dep, n_tail).astype(kind)

    tail_shape = (n_dep, cols // n_dep, n_tail)
    return pl.pallas_call(
        body,
        grid=(steps,),
        in_specs=[
            pl.BlockSpec((block, cols), lambda i: (i + skipped, 0)),
            pl.BlockSpec((n_tail, cols), lambda i: (0, 0)),
        ],
        out_specs=[pl.BlockSpec((cols // parts, block), lambda i: (0, i))] * parts + [whole(tail_shape)],
        out_shape=[jax.ShapeDtypeStruct((cols // parts, n_main), kind)] * parts
        + [jax.ShapeDtypeStruct(tail_shape, kind)],
        compiler_params=params(),
        cost_estimate=cost(),
    )(in_hbm(lower_rows), in_hbm(lower_rows))


def split_states(product, per_block, parts):
    states, width = product.shape
    by_owner = product.reshape(per_block, parts, states // per_block // parts, width)
    return [by_owner[:, i].reshape(states // parts, width) for i in range(parts)]


def rows_product(got, upper_rows, first, block, so_far, per_block, parts):
    k, states = got.shape
    width = upper_rows.shape[1]
    steps = k // block

    def body(low, up, *refs):
        outs, total = refs[-1 - parts : -1], refs[-1]
        i = pl.program_id(0)
        term = dot(low[...].T, up[...])

        @pl.when(i == 0)
        def _():
            total[...] = term

        @pl.when(i > 0)
        def _():
            total[...] += term

        @pl.when(i == steps - 1)
        def _():
            for j, part in enumerate(split_states(total[...], per_block, parts)):
                outs[j][...] = part + refs[j][...] if so_far else part

    shape = (states // parts, width)
    return pl.pallas_call(
        body,
        grid=(steps,),
        in_specs=[
            pl.BlockSpec((block, states), lambda i: (i, 0)),
            pl.BlockSpec((block, width), lambda i: (i + first // block, 0)),
        ]
        + [whole(shape)] * len(so_far),
        out_specs=[whole(shape)] * parts,
        out_shape=[jax.ShapeDtypeStruct(shape, jnp.float32)] * parts,
        scratch_shapes=[pltpu.VMEM((states, width), jnp.float32)],
        compiler_params=params(),
        cost_estimate=cost(),
    )(got, in_hbm(upper_rows), *so_far)


def held_rows(rows, first, k):
    width = rows.shape[1]

    def body(up, out, sem):
        copy = pltpu.make_async_copy(up.at[pl.ds(first, k)], out, sem)
        copy.start()
        copy.wait()

    return pl.pallas_call(
        body,
        in_specs=[pl.BlockSpec(memory_space=pltpu.HBM)],
        out_specs=pl.BlockSpec(memory_space=pltpu.VMEM),
        out_shape=pltpu.VMEM((k, width), rows.dtype),
        scratch_shapes=[pltpu.SemaphoreType.DMA],
        compiler_params=params(),
        cost_estimate=cost(),
    )(in_hbm(rows))


def turned_products(me, core, own, so_far, got, rows, n_core):
    n_up = 1 + len(got)
    states, k = got[0].shape
    width = rows.shape[1]
    steps = 1
    block = k // steps
    share = states // n_core

    def body(me_at, core_at, mine, up, *refs):
        befores, lows_at = refs[: n_up - 1], refs[n_up - 1 : 2 * n_up - 2]
        outs = refs[2 * n_up - 2 : 2 * n_up - 2 + n_core]
        lows, sems = refs[2 * n_up - 2 + n_core :]

        def start(source, target, sem):
            copy = pltpu.make_async_copy(source, target, sem)
            copy.start()
            return copy

        copies = []
        for j in range(steps):
            span = pl.ds(j * block, block)
            copies.append(
                [start(low.at[:, span], lows.at[i, j], sems.at[i, j]) for i, low in enumerate(lows_at)]
            )

        def put(slot, product):
            by_core = product.reshape(n_core, share, width)
            for c in range(n_core):
                for t, out in enumerate(outs):

                    @pl.when(lax.rem(core_at[0] + t, n_core) == c)
                    def _():
                        out[slot] = by_core[c]

        put(me_at[0], mine[...])
        totals = [before[...] for before in befores]
        for j, group in enumerate(copies):
            for copy in group:
                copy.wait()
            totals = [total + dot(lows[i, j], up[j * block : (j + 1) * block]) for i, total in enumerate(totals)]
        for i, total in enumerate(totals):
            put(lax.rem(me_at[0] + 1 + i, n_up), total)

    vmem, hbm = pl.BlockSpec(memory_space=pltpu.VMEM), pl.BlockSpec(memory_space=pltpu.HBM)
    return pl.pallas_call(
        body,
        in_specs=[pl.BlockSpec(memory_space=pltpu.SMEM)] * 2 + [vmem] * (n_up + 1) + [hbm] * (n_up - 1),
        out_specs=[vmem] * n_core,
        out_shape=[jax.ShapeDtypeStruct((n_up, share, width), jnp.float32)] * n_core,
        scratch_shapes=[
            pltpu.VMEM((n_up - 1, steps, states, block), got[0].dtype),
            pltpu.SemaphoreType.DMA((n_up - 1, steps)),
        ],
        compiler_params=params(),
        cost_estimate=cost(),
    )(me.reshape(1), core.reshape(1), own, in_vmem(rows), *so_far, *got)


def tail_product(depth, got, own, forward, backward):
    n_dep, states, k = got.shape
    width = own.shape[1]
    n = n_dep - 1

    def body(at, low, mid, *refs):
        out, lows, ups, sems = refs[2 * n :]
        z = at[0]
        of_low = pltpu.make_async_copy(low, lows, sems.at[n_dep])
        of_low.start()
        copies = [pltpu.make_async_copy(mid, ups.at[0], sems.at[0])]
        copies[0].start()
        for j in range(1, n_dep):
            down = pltpu.make_async_copy(refs[n + j - 1], ups.at[j], sems.at[j])
            round_ = pltpu.make_async_copy(refs[n - j], ups.at[j], sems.at[j])
            pl.when(z + j < n_dep)(down.start)
            pl.when(z + j >= n_dep)(round_.start)
            copies.append(down)
        of_low.wait()
        total = jnp.zeros((states, width), jnp.float32)
        for j, copy in enumerate(copies):
            copy.wait()
            total = total + dot(lows[lax.rem(z + j, n_dep)], ups[j])
        out[...] = total

    hbm = pl.BlockSpec(memory_space=pltpu.HBM)
    return pl.pallas_call(
        body,
        in_specs=[pl.BlockSpec(memory_space=pltpu.SMEM)] + [hbm] * (2 + 2 * n),
        out_specs=pl.BlockSpec(memory_space=pltpu.VMEM),
        out_shape=jax.ShapeDtypeStruct((states, width), jnp.float32),
        scratch_shapes=[
            pltpu.VMEM((n_dep, states, k), got.dtype),
            pltpu.VMEM((n_dep, k, width), own.dtype),
            pltpu.SemaphoreType.DMA((n_dep + 1,)),
        ],
        compiler_params=params(),
        cost_estimate=cost(),
    )(depth.reshape(1), got, own, *forward, *backward)


def finished(from_a, from_b, terms, cubed, weight, mask):
    _, half, width = from_a.shape

    def body(a, b, cube, scale, keep, *refs):
        out = refs[-1]
        tail = refs[0][...]
        for ref in refs[1:-1]:
            tail = tail + ref[...]
        for part, sums in enumerate((jnp.sum(a[...], axis=0), jnp.sum(b[...], axis=0))):
            rows = slice(part * half, (part + 1) * half)
            total = sums + tail[rows]
            value = cube[rows] * (total * total) / scale[...]
            out[rows] = jnp.where(keep[rows] > 0, value, jnp.zeros_like(value))

    vmem = pl.BlockSpec(memory_space=pltpu.VMEM)
    return pl.pallas_call(
        body,
        in_specs=[vmem] * (5 + len(terms)),
        out_specs=vmem,
        out_shape=jax.ShapeDtypeStruct((2 * half, width), jnp.float32),
        compiler_params=params(),
        cost_estimate=cost(),
    )(from_a, from_b, cubed, weight, mask, *terms)


def make_local(n_low, n_up, n_dep):
    n_core = n_low // n_up
    others = range(1, n_up)
    same_core = [[(y * n_core + c) * n_dep + z for y in range(n_up) for z in range(n_dep)] for c in range(n_core)]

    def shifted(x, shift):
        return lax.ppermute(x, "upper", [((u + shift) % n_up, u) for u in range(n_up)])

    def low(y, c):
        return (y % n_up) * n_core + c

    def local(
        lower_vectors, upper_vectors, energy_lower, energy_upper, sym_lower, sym_upper, j_lower, j_upper
    ):
        lower_rows = lower_vectors[0]
        upper_rows = upper_vectors[0]
        rows, cols = lower_rows.shape
        width = upper_rows.shape[1]
        mine = energy_lower.shape[0]
        per_block = cols // mine
        unit = rows // 64
        n_tail, n_head, n_main = 9 * unit, 7 * unit, 48 * unit
        half = mine // 2
        me = lax.axis_index("upper")
        depth = lax.axis_index("depth")
        my_low = lax.axis_index("lower")
        my_y, my_core = my_low // n_core, my_low % n_core

        parity = sym_lower % 2
        sym_rule = sym_upper[None, :] - sym_lower[:, None] == (1 - 2 * parity)[:, None]
        j_rule = jnp.abs(j_upper[None, :] - j_lower[:, None]) <= 1
        allowed = jnp.logical_and(sym_rule, j_rule)
        frequency = energy_upper[None, :] - energy_lower[:, None]
        weight_upper = (2 * j_upper + 1).astype(jnp.float32)
        cubed = frequency * frequency * frequency

        crossed = []

        def cross(x, *others_first):
            if len(crossed) > 1:
                x = after(x, *crossed[-2], *others_first)
            crossed.append([shifted(x, s) for s in others])

        up = [(z, z + 1) for z in range(n_dep - 1)]
        down = [(z + 1, z) for z in range(n_dep - 1)]
        forward, backward = [], []

        def pass_on(held_up, held_down):
            i = len(forward)
            forward.append(lax.ppermute(held_up, "depth", up[i:]))
            backward.append(lax.ppermute(held_down, "depth", down[: n_dep - 1 - i]))

        first = lower_rows[n_tail : n_tail + n_head]
        cross(first)
        later_rows = after(lower_rows, first)
        *turned, tail_rows = turn(later_rows, n_tail, n_main, 2, mine, n_dep)
        cross(turned[0])
        up_tail = after(upper_rows[:n_tail], *crossed[0])
        pass_on(up_tail, up_tail)
        sorted_tail = lax.all_to_all(tail_rows, "depth", 0, 0)
        own = rows_product(after(later_rows, turned[0]), upper_rows, 0, rows // 4, (), per_block, 2)
        cross(turned[1])
        head_rows = upper_rows[n_tail : n_tail + n_head]
        so_far = [rows_product(g, head_rows, 0, n_head, (), per_block, 2) for g in crossed[0]]
        for i in range(1, n_dep - 1):
            held = (forward[-1], backward[-1])
            pass_on(*(after(held, *own, *so_far[0]) if i == 1 else held))

        def reduced(i, got, main_held, *others_first):
            mine_of, *for_others = turned_products(me, my_core, own[i], [x[i] for x in so_far], got, main_held, n_core)
            total = mine_of
            for k, leaving in enumerate(for_others, 1):
                pairs = [(low(y, c), low(y, (c + k) % n_core)) for y in range(n_up) for c in range(n_core)]
                total = total + lax.ppermute(leaving, "lower", pairs)
            total = after(total, *others_first)
            by_owner = total.reshape(n_up * n_dep, half, width)
            return total, lax.all_to_all(by_owner, OWNERS, 0, 0, axis_index_groups=same_core)

        held_a = held_rows(after(upper_rows, *so_far[0]), rows - n_main, n_main)
        sent_a, from_a = reduced(0, crossed[1], held_a, sorted_tail)
        held_b = held_rows(after(upper_rows, from_a), rows - n_main, n_main)
        cross(sorted_tail, from_a)
        last, from_b = reduced(1, crossed[2], held_b, from_a)

        terms = [tail_product(depth, after(g, last), up_tail, forward, backward) for g in crossed[3]]

        def term_for(y):
            block = jnp.zeros_like(terms[0])
            for s in others:
                block = jnp.where((me + s) % n_up == y % n_up, terms[s - 1], block)
            return block

        ends = []
        for t in reversed(range(n_up)):
            by_core = term_for(my_y + t).reshape(n_core, mine, width)
            for k in reversed(range(n_core)):
                term = lax.dynamic_index_in_dim(by_core, (my_core + k) % n_core, 0, keepdims=False)
                if t or k:
                    pairs = [(low(y, c), low(y + t, (c + k) % n_core)) for y in range(n_up) for c in range(n_core)]
                    term = lax.ppermute(term, "lower", pairs)
                ends.append(term)
        return finished(from_a, from_b, ends, cubed, weight_upper[None, :], allowed.astype(jnp.int32))

    return local


def solution(mesh):
    return jax.shard_map(
        make_local(mesh.shape["lower"], mesh.shape["upper"], mesh.shape["depth"]),
        mesh=mesh,
        in_specs=(
            P("depth", "lower", "upper"),
            P("depth", "lower", "upper"),
            P(("lower", "depth")),
            P("upper"),
            P(("lower", "depth")),
            P("upper"),
            P(("lower", "depth")),
            P("upper"),
        ),
        out_specs=P(("lower", "depth"), "upper"),
        check_vma=False,
    )
```

```python
import jax
import jax.numpy as jnp
from jax import lax
from jax.experimental import pallas as pl
from jax.experimental.pallas import tpu as pltpu
from jax.sharding import PartitionSpec as P

OWNERS = ("lower", "depth")
VMEM_LIMIT = 16 * 1024 * 1024


def params():
    return pltpu.CompilerParams(vmem_limit_bytes=VMEM_LIMIT)


def cost():
    return pl.CostEstimate(flops=0, bytes_accessed=30000, transcendentals=0)


def dot(a, b):
    return jnp.dot(a, b, preferred_element_type=jnp.float32)


def after(x, *others):
    return lax.optimization_barrier((x,) + others)[0]


def in_hbm(x):
    return pltpu.with_memory_space_constraint(x, pltpu.HBM)


def in_vmem(x):
    return pltpu.with_memory_space_constraint(x, pltpu.VMEM)


def whole(shape):
    return pl.BlockSpec(shape, lambda *_: (0,) * len(shape))


def turn(lower_rows, n_tail, n_main, parts, mine, n_dep):
    rows, cols = lower_rows.shape
    per_block = cols // mine
    kind = lower_rows.dtype
    steps = 6
    block = n_main // steps
    skipped = (rows - n_main) // block

    def body(low, low_tail, *outs):
        flipped = low[...].astype(jnp.float32).T
        for out, part in zip(outs, split_states(flipped, per_block, parts)):
            out[...] = part.astype(kind)

        @pl.when(pl.program_id(0) == steps - 1)
        def _():
            by_depth = low_tail[...].astype(jnp.float32).T.reshape(per_block // n_dep, n_dep, mine, n_tail)
            for z in range(n_dep):
                outs[-1][z] = by_depth[:, z].reshape(cols // n_dep, n_tail).astype(kind)

    tail_shape = (n_dep, cols // n_dep, n_tail)
    return pl.pallas_call(
        body,
        grid=(steps,),
        in_specs=[
            pl.BlockSpec((block, cols), lambda i: (i + skipped, 0)),
            pl.BlockSpec((n_tail, cols), lambda i: (0, 0)),
        ],
        out_specs=[pl.BlockSpec((cols // parts, block), lambda i: (0, i))] * parts + [whole(tail_shape)],
        out_shape=[jax.ShapeDtypeStruct((cols // parts, n_main), kind)] * parts
        + [jax.ShapeDtypeStruct(tail_shape, kind)],
        compiler_params=params(),
        cost_estimate=cost(),
    )(in_hbm(lower_rows), in_hbm(lower_rows))


def split_states(product, per_block, parts):
    states, width = product.shape
    by_owner = product.reshape(per_block, parts, states // per_block // parts, width)
    return [by_owner[:, i].reshape(states // parts, width) for i in range(parts)]


def rows_product(got, upper_rows, first, block, so_far, per_block, parts):
    k, states = got.shape
    width = upper_rows.shape[1]
    steps = k // block

    def body(low, up, *refs):
        outs, total = refs[-1 - parts : -1], refs[-1]
        i = pl.program_id(0)
        term = dot(low[...].T, up[...])

        @pl.when(i == 0)
        def _():
            total[...] = term

        @pl.when(i > 0)
        def _():
            total[...] += term

        @pl.when(i == steps - 1)
        def _():
            for j, part in enumerate(split_states(total[...], per_block, parts)):
                outs[j][...] = part + refs[j][...] if so_far else part

    shape = (states // parts, width)
    return pl.pallas_call(
        body,
        grid=(steps,),
        in_specs=[
            pl.BlockSpec((block, states), lambda i: (i, 0)),
            pl.BlockSpec((block, width), lambda i: (i + first // block, 0)),
        ]
        + [whole(shape)] * len(so_far),
        out_specs=[whole(shape)] * parts,
        out_shape=[jax.ShapeDtypeStruct(shape, jnp.float32)] * parts,
        scratch_shapes=[pltpu.VMEM((states, width), jnp.float32)],
        compiler_params=params(),
        cost_estimate=cost(),
    )(got, in_hbm(upper_rows), *so_far)


def held_rows(rows, first, k):
    width = rows.shape[1]

    def body(up, out, sem):
        copy = pltpu.make_async_copy(up.at[pl.ds(first, k)], out, sem)
        copy.start()
        copy.wait()

    return pl.pallas_call(
        body,
        in_specs=[pl.BlockSpec(memory_space=pltpu.HBM)],
        out_specs=pl.BlockSpec(memory_space=pltpu.VMEM),
        out_shape=pltpu.VMEM((k, width), rows.dtype),
        scratch_shapes=[pltpu.SemaphoreType.DMA],
        compiler_params=params(),
        cost_estimate=cost(),
    )(in_hbm(rows))


def turned_products(me, core, own, so_far, got, rows, n_core, n_dep):
    n_up = 1 + len(got)
    states, k = got[0].shape
    width = rows.shape[1]
    steps = 1
    block = k // steps
    share = states // n_core

    def body(me_at, core_at, mine, up, *refs):
        befores, lows_at = refs[: n_up - 1], refs[n_up - 1 : 2 * n_up - 2]
        outs = refs[2 * n_up - 2 : 2 * n_up - 2 + n_core]
        lows, sems = refs[2 * n_up - 2 + n_core :]

        def start(source, target, sem):
            copy = pltpu.make_async_copy(source, target, sem)
            copy.start()
            return copy

        copies = []
        for j in range(steps):
            span = pl.ds(j * block, block)
            copies.append(
                [start(low.at[:, span], lows.at[i, j], sems.at[i, j]) for i, low in enumerate(lows_at)]
            )

        def put(slot, product):
            by_core = product.reshape(n_core, n_dep, share // n_dep, width)
            for c in range(n_core):
                for t, out in enumerate(outs):

                    @pl.when(lax.rem(core_at[0] + t, n_core) == c)
                    def _():
                        out[:, slot] = by_core[c]

        put(me_at[0], mine[...])
        totals = [before[...] for before in befores]
        for j, group in enumerate(copies):
            for copy in group:
                copy.wait()
            totals = [total + dot(lows[i, j], up[j * block : (j + 1) * block]) for i, total in enumerate(totals)]
        for i, total in enumerate(totals):
            put(lax.rem(me_at[0] + 1 + i, n_up), total)

    vmem, hbm = pl.BlockSpec(memory_space=pltpu.VMEM), pl.BlockSpec(memory_space=pltpu.HBM)
    return pl.pallas_call(
        body,
        in_specs=[pl.BlockSpec(memory_space=pltpu.SMEM)] * 2 + [vmem] * (n_up + 1) + [hbm] * (n_up - 1),
        out_specs=[vmem] * n_core,
        out_shape=[jax.ShapeDtypeStruct((n_dep, n_up, share // n_dep, width), jnp.float32)] * n_core,
        scratch_shapes=[
            pltpu.VMEM((n_up - 1, steps, states, block), got[0].dtype),
            pltpu.SemaphoreType.DMA((n_up - 1, steps)),
        ],
        compiler_params=params(),
        cost_estimate=cost(),
    )(me.reshape(1), core.reshape(1), own, in_vmem(rows), *so_far, *got)


def tail_product(depth, got, own, forward, backward):
    n_dep, states, k = got.shape
    width = own.shape[1]
    n = n_dep - 1

    def body(at, low, mid, *refs):
        out, lows, ups, sems = refs[2 * n :]
        z = at[0]
        of_low = pltpu.make_async_copy(low, lows, sems.at[n_dep])
        of_low.start()
        copies = [pltpu.make_async_copy(mid, ups.at[0], sems.at[0])]
        copies[0].start()
        for j in range(1, n_dep):
            down = pltpu.make_async_copy(refs[n + j - 1], ups.at[j], sems.at[j])
            round_ = pltpu.make_async_copy(refs[n - j], ups.at[j], sems.at[j])
            pl.when(z + j < n_dep)(down.start)
            pl.when(z + j >= n_dep)(round_.start)
            copies.append(down)
        of_low.wait()
        total = jnp.zeros((states, width), jnp.float32)
        for j, copy in enumerate(copies):
            copy.wait()
            total = total + dot(lows[lax.rem(z + j, n_dep)], ups[j])
        out[...] = total

    hbm = pl.BlockSpec(memory_space=pltpu.HBM)
    return pl.pallas_call(
        body,
        in_specs=[pl.BlockSpec(memory_space=pltpu.SMEM)] + [hbm] * (2 + 2 * n),
        out_specs=pl.BlockSpec(memory_space=pltpu.VMEM),
        out_shape=jax.ShapeDtypeStruct((states, width), jnp.float32),
        scratch_shapes=[
            pltpu.VMEM((n_dep, states, k), got.dtype),
            pltpu.VMEM((n_dep, k, width), own.dtype),
            pltpu.SemaphoreType.DMA((n_dep + 1,)),
        ],
        compiler_params=params(),
        cost_estimate=cost(),
    )(depth.reshape(1), got, own, *forward, *backward)


def make_local(n_low, n_up, n_dep):
    n_core = n_low // n_up
    others = range(1, n_up)
    same_core = [[(y * n_core + c) * n_dep + z for z in range(n_dep) for y in range(n_up)] for c in range(n_core)]

    def shifted(x, shift):
        return lax.ppermute(x, "upper", [((u + shift) % n_up, u) for u in range(n_up)])

    def low(y, c):
        return (y % n_up) * n_core + c

    def local(
        lower_vectors, upper_vectors, energy_lower, energy_upper, sym_lower, sym_upper, j_lower, j_upper
    ):
        lower_rows = lower_vectors[0]
        upper_rows = upper_vectors[0]
        rows, cols = lower_rows.shape
        width = upper_rows.shape[1]
        mine = energy_lower.shape[0]
        per_block = cols // mine
        unit = rows // 64
        n_tail, n_head, n_main = 9 * unit, 7 * unit, 48 * unit
        half = mine // 2
        me = lax.axis_index("upper")
        depth = lax.axis_index("depth")
        my_low = lax.axis_index("lower")
        my_y, my_core = my_low // n_core, my_low % n_core

        parity = sym_lower % 2
        sym_rule = sym_upper[None, :] - sym_lower[:, None] == (1 - 2 * parity)[:, None]
        j_rule = jnp.abs(j_upper[None, :] - j_lower[:, None]) <= 1
        allowed = jnp.logical_and(sym_rule, j_rule)
        frequency = energy_upper[None, :] - energy_lower[:, None]
        weight_upper = (2 * j_upper + 1).astype(jnp.float32)
        cubed = frequency * frequency * frequency

        crossed = []

        def cross(x, *others_first):
            if len(crossed) > 1:
                x = after(x, *crossed[-2], *others_first)
            crossed.append([shifted(x, s) for s in others])

        up = [(z, z + 1) for z in range(n_dep - 1)]
        down = [(z + 1, z) for z in range(n_dep - 1)]
        forward, backward = [], []

        def pass_on(held_up, held_down):
            i = len(forward)
            forward.append(lax.ppermute(held_up, "depth", up[i:]))
            backward.append(lax.ppermute(held_down, "depth", down[: n_dep - 1 - i]))

        first = lower_rows[n_tail : n_tail + n_head]
        cross(first)
        later_rows = after(lower_rows, first)
        *turned, tail_rows = turn(later_rows, n_tail, n_main, 2, mine, n_dep)
        cross(turned[0])
        up_tail = after(upper_rows[:n_tail], *crossed[0])
        pass_on(up_tail, up_tail)
        sorted_tail = lax.all_to_all(tail_rows, "depth", 0, 0)
        own = rows_product(after(later_rows, turned[0]), upper_rows, 0, rows // 4, (), per_block, 2)
        cross(turned[1])
        head_rows = upper_rows[n_tail : n_tail + n_head]
        so_far = [rows_product(g, head_rows, 0, n_head, (), per_block, 2) for g in crossed[0]]
        for i in range(1, n_dep - 1):
            held = (forward[-1], backward[-1])
            pass_on(*(after(held, *own, *so_far[0]) if i == 1 else held))

        def reduced(i, got, main_held, *others_first):
            mine_of, *for_others = turned_products(me, my_core, own[i], [x[i] for x in so_far], got, main_held, n_core, n_dep)
            total = mine_of
            for k, leaving in enumerate(for_others, 1):
                pairs = [(low(y, c), low(y, (c + k) % n_core)) for y in range(n_up) for c in range(n_core)]
                total = total + lax.ppermute(leaving, "lower", pairs)
            total = after(total, *others_first)
            by_owner = total.reshape(n_up * n_dep, half, width)
            return total, lax.all_to_all(by_owner, OWNERS, 0, 0, axis_index_groups=same_core)

        held_a = held_rows(after(upper_rows, *so_far[0]), rows - n_main, n_main)
        sent_a, from_a = reduced(0, crossed[1], held_a, sorted_tail)
        held_b = held_rows(after(upper_rows, sent_a), rows - n_main, n_main)
        cross(sorted_tail, from_a)
        last, from_b = reduced(1, crossed[2], held_b, from_a)
        sum_a, sum_b = jnp.sum(from_a, axis=0), jnp.sum(from_b, axis=0)
        main = jnp.concatenate([sum_a, sum_b], axis=0)

        terms = [tail_product(depth, after(g, last), up_tail, forward, backward) for g in crossed[3]]

        def term_for(y):
            block = jnp.zeros_like(terms[0])
            for s in others:
                block = jnp.where((me + s) % n_up == y % n_up, terms[s - 1], block)
            return block

        total = main
        for t in reversed(range(n_up)):
            by_core = term_for(my_y + t).reshape(n_core, mine, width)
            for k in reversed(range(n_core)):
                term = lax.dynamic_index_in_dim(by_core, (my_core + k) % n_core, 0, keepdims=False)
                if t or k:
                    pairs = [(low(y, c), low(y + t, (c + k) % n_core)) for y in range(n_up) for c in range(n_core)]
                    term = lax.ppermute(term, "lower", pairs)
                total = total + term
        value = cubed * (total * total) / weight_upper[None, :]
        return jnp.where(allowed, value, jnp.zeros_like(value))

    return local


def solution(mesh):
    return jax.shard_map(
        make_local(mesh.shape["lower"], mesh.shape["upper"], mesh.shape["depth"]),
        mesh=mesh,
        in_specs=(
            P("depth", "lower", "upper"),
            P("depth", "lower", "upper"),
            P(("lower", "depth")),
            P("upper"),
            P(("lower", "depth")),
            P("upper"),
            P(("lower", "depth")),
            P("upper"),
        ),
        out_specs=P(("lower", "depth"), "upper"),
        check_vma=False,
    )
```
